256 devices in a mesh: pair: 2 (over x_lo), ep: 128 (over x_hi, y, z, core).
Axes of the slice: x: 4 (x_hi: 2, x_lo: 2; x = x_hi * 2 + x_lo), y: 4, z: 8, core: 2. Of those that a mesh axis runs over, the one named last changes fastest.
Arguments:
- tokens: bfloat16 [256, 256, 1280], P(('pair', 'ep')), may hold values from -48 to 48
- slot_params: bfloat16 [1280, 128], replicated, may hold values from -1 to 1
- slot_outputs: bfloat16 [256, 128, 1280], P(('pair', 'ep')), may hold values from -1.5 to 1.5
- expert_inputs: bfloat16 [128, 256, 1280], P('ep'), may hold values from -6 to 6
- w_in: bfloat16 [128, 1280, 2560], P('ep', None, 'pair'), may hold values from -0.15625 to 0.15625
- w_out: bfloat16 [128, 2560, 1280], P('ep', 'pair'), may hold values from -0.125 to 0.125
- cotangent: bfloat16 [256, 256, 1280], P(('pair', 'ep')), may hold values from -48 to 48
Outputs:
- d_tokens: bfloat16 [256, 256, 1280], P(('pair', 'ep'))
- d_slot_params: float32 [1280, 128], P(('pair', 'ep'))
- d_w_in: bfloat16 [128, 1280, 2560], P('ep', None, 'pair')
The draws below stay inside these ranges and needn't reach their ends.
All inputs are finite; a program needn't handle non-finite values.
Results may differ from the reference program's by a relative error of at most 0.011.
Values may be sent and summed in bfloat16 or wider, within the bound.
A program may use at most 64 MiB of HBM per device.

```python
import jax
import jax.numpy as jnp
from jax import lax

D = 1280
HID = 2560
M = 256
EXPERTS = 128
IMAGES = 256


def phi_base(key):
    return jnp.clip(jax.random.normal(key, (D, EXPERTS), jnp.float32), -6.0, 6.0)


def draw_slot_params(key, part):
    base = phi_base(key)
    return (base * D ** (-0.5)).astype(jnp.bfloat16)


def draw_tokens(key, part):
    key = jax.random.fold_in(key, 7)
    whole = jnp.clip(jax.random.normal(key, (IMAGES, M, D), jnp.float32), -6.0, 6.0)
    return whole.astype(jnp.bfloat16)


def block_levels(own_key, dims, shards, least, high):
    def one(position, shards_of):
        draws = jax.random.uniform(jax.random.fold_in(jax.random.fold_in(own_key, 6), position), (shards_of,), jnp.float32, least / len(shards), high / len(shards))
        return jnp.repeat(jnp.exp(draws), dims[position] // shards_of).reshape((-1,) + (1,) * (len(dims) - position - 1))

    factor_of = one(*shards[0])
    for cut in shards[1:]:
        factor_of = factor_of * one(*cut)
    return factor_of


def scatter_about(stream_key, dims, deviation, limit, pieces=(), kind=jnp.bfloat16):
    values = jax.random.normal(stream_key, dims, jnp.float32) * deviation
    if len(pieces) > 0:
        values = block_levels(stream_key, dims, pieces, -0.22, 0.18) * values
    return jnp.clip(values, min=-limit, max=limit).astype(kind)


def setup_inputs(seed: int = 0) -> dict:
    seeds = jax.random.split(jax.random.key(seed), 8)
    tokens = draw_tokens(jax.random.fold_in(seeds[7], 71), 0)
    slot_params = draw_slot_params(jax.random.fold_in(seeds[7], 71), 0)
    slot_outputs = scatter_about(seeds[2], (IMAGES, EXPERTS, D), 0.25, 1.5, ((0, 256),))
    expert_inputs = scatter_about(seeds[3], (EXPERTS, IMAGES, D), 1.0, 6.0, ((0, 128),))
    w_in = scatter_about(seeds[4], (EXPERTS, D, HID), D ** -0.5, 0.15625, ((0, 128), (2, 2)))
    w_out = scatter_about(seeds[5], (EXPERTS, HID, D), HID ** -0.5, 0.125, ((0, 128), (1, 2)))
    cotangent = scatter_about(seeds[6], (IMAGES, M, D), 8.0, 48.0, ((0, 256),))
    return dict(tokens=tokens, slot_params=slot_params, slot_outputs=slot_outputs, expert_inputs=expert_inputs, w_in=w_in, w_out=w_out, cotangent=cotangent)


def exact_gelu(value):
    return jax.nn.gelu(value, approximate=False)

def gelu_back(pre, d_act):
    return jax.vjp(exact_gelu, pre)[1](d_act)[0]

def expert_back(inputs):
    rows, grads, first, second = inputs
    pre = jnp.dot(rows, first, preferred_element_type=jnp.float32)
    d_act = jnp.dot(grads, second.T, preferred_element_type=jnp.float32)
    d_pre = gelu_back(pre, d_act).astype(jnp.bfloat16)
    d_first = jnp.dot(rows.T, d_pre, preferred_element_type=jnp.float32).astype(jnp.bfloat16)
    d_rows = jnp.dot(d_pre, first.T, preferred_element_type=jnp.float32).astype(jnp.bfloat16)
    return (d_first, d_rows)

def reference(tokens, slot_params, slot_outputs, expert_inputs, w_in, w_out, cotangent):
    tok32 = tokens.astype(jnp.float32)
    cot32 = cotangent.astype(jnp.float32)
    phi32 = slot_params.astype(jnp.float32)
    logits = jnp.einsum('imd,ds->ims', tok32, phi32)
    dispatch = jax.nn.softmax(logits, axis=1)
    combine = jax.nn.softmax(logits, axis=2)
    dispatch_b = dispatch.astype(jnp.bfloat16)
    combine_b = combine.astype(jnp.bfloat16)
    d_slot_out = jnp.einsum('ims,imd->isd', combine_b.astype(jnp.float32), cot32).astype(jnp.bfloat16)
    d_w_in, d_slot_in = lax.map(expert_back, (expert_inputs, jnp.swapaxes(d_slot_out, 0, 1), w_in, w_out))
    back = jnp.swapaxes(d_slot_in, 0, 1).astype(jnp.float32)
    d_disp = jnp.einsum('imd,isd->ims', tok32, back)
    d_comb = jnp.einsum('imd,isd->ims', cot32, slot_outputs.astype(jnp.float32))
    d_logits = dispatch * (d_disp - lax.optimization_barrier(jnp.sum(dispatch * d_disp, axis=1, keepdims=True)))
    d_logits = d_logits + combine * (d_comb - lax.optimization_barrier(jnp.sum(combine * d_comb, axis=2, keepdims=True)))
    d_logits_b = d_logits.astype(jnp.bfloat16).astype(jnp.float32)
    d_tokens = jnp.einsum('ims,isd->imd', dispatch_b.astype(jnp.float32), back) + jnp.einsum('ims,ds->imd', d_logits_b, phi32)
    d_slot_params = jnp.einsum('imd,ims->ds', tok32, d_logits_b)
    return (d_tokens.astype(jnp.bfloat16), d_slot_params, d_w_in)
```

```python
import functools

import jax
import jax.numpy as jnp
from jax import lax
from jax.experimental import pallas as pl
from jax.experimental.pallas import tpu as pltpu
from jax.sharding import PartitionSpec as P

F32 = jnp.float32
BF16 = jnp.bfloat16
MESH = pl.DeviceIdType.MESH

NX, NY, NZ, NC = 2, 4, 8, 2
NYC = NY * NC
PLANE = NY * NZ * NC
SLOTS = NX * PLANE
CHUNKS = 5
VMEM_LIMIT = 56 * 2**20

Z1, Y1, N1, P1, R1, P2, N2, Y2, Z2, SC, SY, SX, SF = range(13)


def dot_nn(a, b):
    return lax.dot_general(a, b, (((1,), (0,)), ((), ())), preferred_element_type=F32)


def dot_nt(a, b):
    return lax.dot_general(a, b, (((1,), (1,)), ((), ())), preferred_element_type=F32)


def dot_tn(a, b):
    return lax.dot_general(a, b, (((0,), (0,)), ((), ())), preferred_element_type=F32)


def log2(n):
    return n.bit_length() - 1


def digits(value, sizes):
    out = []
    for size in reversed(sizes):
        out.append(value & (size - 1))
        value = value >> log2(size)
    return out[::-1]


def number(values, sizes):
    total = None
    for value, size in zip(values, sizes):
        total = value if total is None else (total << log2(size)) + value
    return total


def one_hot(source, along):
    r = lax.broadcasted_iota(jnp.int32, (SLOTS, SLOTS), along)
    other = lax.broadcasted_iota(jnp.int32, (SLOTS, SLOTS), 1 - along)
    return jnp.where(source(r) == other, 1.0, 0.0).astype(BF16)


def slot_of_place(r):
    z, h, y, c = digits(r, (NZ, NX, NY, NC))
    return number((h, y, z, c), (NX, NY, NZ, NC))


def turn_source(r):
    yc, h, z = digits(r, (NYC, NX, NZ))
    return number((z, h, yc), (NZ, NX, NYC))


def unturn_source(r):
    z, h, yc = digits(r, (NZ, NX, NYC))
    return number((yc, h, z), (NYC, NX, NZ))


def gather_source(r):
    h, y, z, c = digits(r, (NX, NY, NZ, NC))
    return number((y, c, h, z), (NY, NC, NX, NZ))


def permute(matrix, rows):
    return dot_nn(matrix, rows).astype(BF16)


def kernel(
    tok_h, phi_h, so_h, ei_h, win_h, wout_h, cot_h,
    dtok_h, dphi_o, dwin_h,
    tok, phi, so, ei, win, wout, cot,
    phip, sop, gate, act, dpre, disp, comb, dcomb,
    place, turn, unturn, gath,
    sendz, recvz, sendy, recvy, sendn, rows,
    part, sendp, recvp, sumn, both, sendy2, recvy2, sendz2, back,
    dtok, dwin, ddisp, dlog,
    ph, recvc, sumc, sends, recvs, sumy, recvx, sendf, recvf,
    send_sem, recv_sem, load_sem, out_sem,
):
    wide = tok.shape[1]
    cols = wide // CHUNKS
    hid = win.shape[1]
    hcols = hid // CHUNKS
    fine = wide // (2 * SLOTS)
    zrows = NX * NYC
    yrows = NX * NZ

    p = lax.axis_index("pair")
    e = lax.axis_index("ep")
    c = lax.rem(e, NC)
    z = lax.rem(lax.div(e, NC), NZ)
    y = lax.rem(lax.div(e, NC * NZ), NY)
    h = lax.div(e, PLANE)
    yc = y * NC + c

    def at(pair=p, h=h, y=y, z=z, c=c):
        return (pair, h * PLANE + y * (NZ * NC) + z * NC + c)

    partner = at(pair=1 - p)
    near = at(pair=1 - p, h=1 - h)
    far = at(h=1 - h)
    z_peers = []
    for k in range(1, NZ):
        other = lax.rem(z + k, NZ)
        z_peers.append((other, at(z=other)))
    yc_peers = []
    for k in range(1, NYC):
        other = lax.rem(yc + k, NYC)
        yc_peers.append((other, at(y=lax.div(other, NC), c=lax.rem(other, NC))))
    half = lax.div(z, NZ // 2)
    mine = jnp.logical_and(c == p, half == p)

    def remote(src, dst, step, ch, device):
        return pltpu.make_async_remote_copy(
            src_ref=src, dst_ref=dst, send_sem=send_sem.at[step, ch], recv_sem=recv_sem.at[step, ch],
            device_id=device, device_id_type=MESH,
        )

    def arrived(dst, step, ch):
        pltpu.make_async_copy(dst, dst, recv_sem.at[step, ch]).wait()

    def left(src, step, ch):
        pltpu.make_async_copy(src, src, send_sem.at[step, ch]).wait()

    def aligned(start, size):
        return pl.ds(pl.multiple_of(start, size), size)

    loads = [
        pltpu.make_async_copy(src, dst, load_sem.at[k])
        for k, (src, dst) in enumerate(
            [(tok_h, tok), (phi_h, phi), (cot_h, cot), (ei_h, ei), (win_h, win), (so_h, so), (wout_h, wout)]
        )
    ]
    for load in loads:
        load.start()
    load_tok, load_phi, load_cot, load_ei, load_win, load_so, load_wout = loads

    barrier = pltpu.get_barrier_semaphore()
    for device in [q[1] for q in z_peers] + [q[1] for q in yc_peers] + [partner, near, far]:
        pl.semaphore_signal(barrier, inc=1, device_id=device, device_id_type=MESH)
    for k in range(NZ):
        source = at(pair=half, z=k, c=p)

        @pl.when(jnp.logical_not(jnp.logical_and(mine, z == k)))
        def _():
            pl.semaphore_signal(barrier, inc=1, device_id=source, device_id_type=MESH)

    place[...] = one_hot(slot_of_place, 1)
    turn[...] = one_hot(turn_source, 0)
    unturn[...] = one_hot(unturn_source, 0)
    gath[...] = one_hot(gather_source, 0)

    load_phi.wait()
    phip[...] = dot_nn(phi[...], place[...]).astype(BF16)
    load_tok.wait()
    logits = dot_nn(tok[...], phip[...])
    over_tokens = jnp.exp(logits - jnp.max(logits, axis=0, keepdims=True))
    disp[...] = over_tokens / jnp.sum(over_tokens, axis=0, keepdims=True)
    over_slots = jnp.exp(logits - jnp.max(logits, axis=1, keepdims=True))
    combine = over_slots / jnp.sum(over_slots, axis=1, keepdims=True)
    comb[...] = combine
    combine_t = jnp.transpose(combine).astype(BF16)
    load_cot.wait()

    pl.semaphore_wait(barrier, (NZ - 1) + (NYC - 1) + 3 + NZ - jnp.where(mine, 1, 0))

    for ch in range(CHUNKS):
        sendz[ch] = dot_nn(combine_t, cot[:, ch * cols : (ch + 1) * cols]).astype(BF16)
        for other, device in z_peers:
            remote(sendz.at[ch, aligned(other * zrows, zrows)], recvz.at[ch, aligned(z * zrows, zrows)], Z1, ch, device).start()
        own = aligned(z * zrows, zrows)
        recvz[ch, own, :] = sendz[ch, own, :]

    act[...] = jnp.zeros_like(act)
    load_ei.wait()
    load_win.wait()

    def pre_part(ch):
        span = aligned(ch * hcols, hcols)
        pre = dot_nn(ei[...], win[:, span])
        cdf = 0.5 * (1.0 + lax.erf(pre * (0.5**0.5)))
        pdf = jnp.exp(-0.5 * pre * pre) * 0.3989422804014327
        gate[:, span] = cdf + pre * pdf

    def z_arrives(ch):
        arrived(recvz.at[ch, pl.ds(0, SLOTS - zrows)], Z1, ch)
        sendy[ch] = permute(turn[...], recvz[ch])
        for other, device in yc_peers:
            remote(sendy.at[ch, aligned(other * yrows, yrows)], recvy.at[ch, aligned(yc * yrows, yrows)], Y1, ch, device).start()
        own = aligned(yc * yrows, yrows)
        recvy[ch, own, :] = sendy[ch, own, :]

    here = aligned((p * NX + h) * PLANE, PLANE)
    there = aligned(((1 - p) * NX + 1 - h) * PLANE, PLANE)

    def y_arrives(ch):
        arrived(recvy.at[ch, pl.ds(0, SLOTS - yrows)], Y1, ch)
        sendn[ch] = permute(gath[...], recvy[ch])
        own = sendn.at[ch, aligned(h * PLANE, PLANE)]
        remote(sendn.at[ch, aligned((1 - h) * PLANE, PLANE)], rows.at[ch, here], N1, ch, near).start()
        remote(own, rows.at[ch, here], P1, ch, partner).start()
        rows[ch, here, :] = sendn[ch, aligned(h * PLANE, PLANE), :]

    def near_arrives(ch):
        arrived(rows.at[ch, there], N1, ch)
        remote(rows.at[ch, there], rows.at[ch, there], R1, ch, partner).start()

    def all_arrived(ch):
        arrived(rows.at[ch, here], P1, ch)
        arrived(rows.at[ch, here], R1, ch)
        for k in range(CHUNKS):
            span = slice(k * hcols, (k + 1) * hcols)
            act[:, span] += dot_nt(rows[ch], wout[span, aligned(ch * cols, cols)])

    def pipeline(steps, n):
        def body(t, _):
            for lag, step in steps:
                pl.when(jnp.logical_and(t >= lag, t < lag + n))(functools.partial(step, t - lag))
            return 0

        lax.fori_loop(0, n + max(lag for lag, _ in steps), body, 0)

    pre_part(0)
    load_wout.wait()
    pipeline([(0, z_arrives), (1, y_arrives), (2, near_arrives), (3, all_arrived), (-1, pre_part)], CHUNKS)
    load_so.wait()
    sop[...] = dot_tn(place[...], so[...]).astype(BF16)
    dcomb[...] = dot_nt(cot[...], sop[...])
    dpre[...] = (act[...] * gate[...]).astype(BF16)

    def rows_back(ch):
        part[ch] = dot_nt(dpre[...], win[aligned(ch * cols, cols), :])
        sendp[ch, 0:PLANE, :] = part[ch, aligned(((1 - p) * NX + h) * PLANE, PLANE), :].astype(BF16)
        sendp[ch, PLANE : 2 * PLANE, :] = part[ch, aligned((p * NX + 1 - h) * PLANE, PLANE), :].astype(BF16)
        remote(sendp.at[ch], recvp.at[ch], P2, ch, partner).start()

    def pair_arrives(ch):
        arrived(recvp.at[ch], P2, ch)
        sumn[ch] = (part[ch, there, :] + recvp[ch, PLANE : 2 * PLANE, :].astype(F32)).astype(BF16)
        remote(sumn.at[ch], both.at[ch, aligned(h * PLANE, PLANE)], N2, ch, near).start()
        both[ch, aligned(h * PLANE, PLANE), :] = (part[ch, here, :] + recvp[ch, 0:PLANE, :].astype(F32)).astype(BF16)

    def sums_arrive(ch):
        arrived(sumn.at[ch], N2, ch)
        sendy2[ch] = dot_tn(gath[...], both[ch]).astype(BF16)
        for other, device in yc_peers:
            remote(sendy2.at[ch, aligned(other * yrows, yrows)], recvy2.at[ch, aligned(yc * yrows, yrows)], Y2, ch, device).start()
        own = aligned(yc * yrows, yrows)
        recvy2[ch, own, :] = sendy2[ch, own, :]

    def y_arrives_back(ch):
        arrived(recvy2.at[ch, pl.ds(0, SLOTS - yrows)], Y2, ch)
        sendz2[ch] = permute(unturn[...], recvy2[ch])
        for other, device in z_peers:
            remote(sendz2.at[ch, aligned(other * zrows, zrows)], back.at[ch, aligned(z * zrows, zrows)], Z2, ch, device).start()
        own = aligned(z * zrows, zrows)
        back[ch, own, :] = sendz2[ch, own, :]

    def z_arrives_back(ch):
        arrived(back.at[ch, pl.ds(0, SLOTS - zrows)], Z2, ch)
        ddisp[...] += dot_nt(tok[:, aligned(ch * cols, cols)], back[ch])

    def dwin_part(ch):
        span = aligned(ch * cols, cols)
        for k in range(CHUNKS):
            wide_span = slice(k * hcols, (k + 1) * hcols)
            dwin[span, wide_span] = dot_tn(ei[:, span], dpre[:, wide_span]).astype(BF16)
        pltpu.make_async_copy(dwin.at[span], dwin_h.at[span], out_sem.at[ch]).start()

    ddisp[...] = jnp.zeros_like(ddisp)
    pipeline(
        [(0, rows_back), (1, pair_arrives), (2, sums_arrive), (3, y_arrives_back), (2, dwin_part), (4, z_arrives_back)], CHUNKS
    )

    d_disp = ddisp[...]
    d_comb = dcomb[...]
    dispatch = disp[...]
    combine = comb[...]
    d_logits = dispatch * (d_disp - jnp.sum(dispatch * d_disp, axis=0, keepdims=True))
    d_logits = d_logits + combine * (d_comb - jnp.sum(combine * d_comb, axis=1, keepdims=True))
    d_logits = d_logits.astype(BF16)
    dlog[...] = d_logits

    in_order = dot_nt(d_logits, place[...]).astype(BF16)
    ph[...] = dot_tn(tok[...], in_order)
    top = wide // 2
    remote(ph.at[aligned((1 - c) * top, top)], recvc, SC, 0, at(c=1 - c)).start()

    dispatch_b = disp[...].astype(BF16)

    def d_tokens(ch, _):
        span = aligned(ch * cols, cols)
        dtok[:, span] = (dot_nn(dispatch_b, back[ch]) + dot_nt(dlog[...], phip[span, :])).astype(BF16)
        return 0

    lax.fori_loop(0, CHUNKS, d_tokens, 0)
    store_dtok = pltpu.make_async_copy(dtok, dtok_h, out_sem.at[CHUNKS])
    store_dtok.start()

    arrived(recvc, SC, 0)
    sumc[...] = ph[aligned(c * top, top), :] + recvc[...]
    q = top // (NX * NY)
    for other in range(NY):
        for k in range(NX):
            start = (k * NY + other) * q
            sends[other, k * q : (k + 1) * q, :] = sumc[start : start + q, :].astype(BF16)
    for k in range(1, NY):
        other = lax.rem(y + k, NY)
        remote(sends.at[other], recvs.at[k - 1], SY, 0, at(y=other)).start()
    arrived(recvs, SY, 0)
    from_y = recvs[0].astype(F32)
    for k in range(1, NY - 1):
        from_y = from_y + recvs[k].astype(F32)
    for k in range(NX):
        sumy[k * q : (k + 1) * q, :] = sumc[aligned((k * NY + y) * q, q), :] + from_y[k * q : (k + 1) * q, :]
    quarter = q // 2
    for k, device, piece in (
        (0, partner, h * 2 + 1 - p),
        (1, near, (1 - h) * 2 + 1 - p),
        (2, far, (1 - h) * 2 + p),
    ):
        remote(sumy.at[aligned(piece * quarter, quarter)], recvx.at[k], SX, 0, device).start()
    arrived(recvx, SX, 0)
    sumx = sumy[aligned((h * 2 + p) * quarter, quarter), :] + recvx[0] + recvx[1] + recvx[2]
    sendf[...] = jnp.zeros_like(sendf)
    for k in range(NZ):
        sendf[k, 0:fine, :] = sumx[k * fine : (k + 1) * fine, :]
    for k in range(NZ):
        zk, ck = k // NC, k % NC
        is_me = jnp.logical_and(mine, jnp.logical_and(z == p * (NZ // 2) + zk, c == ck))

        @pl.when(is_me)
        def _():
            pltpu.make_async_copy(sendf.at[k], recvf.at[z], recv_sem.at[SF, 0]).start()

        @pl.when(jnp.logical_not(is_me))
        def _():
            remote(sendf.at[k], recvf.at[z], SF, 0, at(pair=c, z=p * (NZ // 2) + zk, c=ck)).start()

    arrived(recvf, SF, 0)
    total = recvf[0]
    for k in range(1, NZ):
        total = total + recvf[k]
    dphi_o[...] = total[0:fine, :]

    def sent(ch, _):
        left(sendz.at[ch, pl.ds(0, SLOTS - zrows)], Z1, ch)
        left(sendy.at[ch, pl.ds(0, SLOTS - yrows)], Y1, ch)
        left(rows.at[ch, here], N1, ch)
        left(rows.at[ch, here], P1, ch)
        left(rows.at[ch, there], R1, ch)
        left(sendp.at[ch], P2, ch)
        left(sumn.at[ch], N2, ch)
        left(sendy2.at[ch, pl.ds(0, SLOTS - yrows)], Y2, ch)
        left(sendz2.at[ch, pl.ds(0, SLOTS - zrows)], Z2, ch)
        span = aligned(ch * cols, cols)
        pltpu.make_async_copy(dwin.at[span], dwin_h.at[span], out_sem.at[ch]).wait()
        return 0

    lax.fori_loop(0, CHUNKS, sent, 0)
    left(recvc, SC, 0)
    left(recvs, SY, 0)
    left(recvx, SX, 0)

    @pl.when(mine)
    def _():
        left(sendf.at[pl.ds(0, NZ - 1)], SF, 0)

    @pl.when(jnp.logical_not(mine))
    def _():
        left(sendf, SF, 0)

    store_dtok.wait()


def per_device(tokens, slot_params, slot_outputs, expert_inputs, w_in, w_out, cotangent):
    images, (m, wide), slots, hid = 2 * SLOTS, tokens.shape[1:], SLOTS, w_in.shape[2]
    cols = wide // CHUNKS
    fine = wide // images
    top = wide // 2
    q = top // (NX * NY)
    vmem = pltpu.VMEM
    scratch = [
        vmem((m, wide), BF16), vmem((wide, slots), BF16), vmem((slots, wide), BF16), vmem((images, wide), BF16),
        vmem((wide, hid), BF16), vmem((hid, wide), BF16), vmem((m, wide), BF16),
        vmem((wide, slots), BF16), vmem((slots, wide), BF16), vmem((images, hid), F32), vmem((images, hid), F32),
        vmem((images, hid), BF16), vmem((m, slots), F32), vmem((m, slots), F32), vmem((m, slots), F32),
        vmem((slots, slots), BF16), vmem((slots, slots), BF16), vmem((slots, slots), BF16), vmem((slots, slots), BF16),
    ]
    block = vmem((CHUNKS, slots, cols), BF16)
    scratch += [block, block, block, block, block, vmem((CHUNKS, images, cols), BF16)]
    scratch += [vmem((CHUNKS, images, cols), F32), block, block, vmem((CHUNKS, PLANE, cols), BF16)]
    scratch += [block, block, block, block, block]
    scratch += [vmem((m, wide), BF16), vmem((wide, hid), BF16), vmem((m, slots), F32), vmem((m, slots), BF16)]
    scratch += [
        vmem((wide, slots), F32), vmem((top, slots), F32), vmem((top, slots), F32),
        vmem((NY, NX * q, slots), BF16), vmem((NY - 1, NX * q, slots), BF16), vmem((NX * q, slots), F32),
        vmem((3, q // 2, slots), F32), vmem((NZ, 8, slots), F32), vmem((NZ, 8, slots), F32),
    ]
    sems = pltpu.SemaphoreType.DMA
    scratch += [sems((13, CHUNKS)), sems((13, CHUNKS)), sems((7,)), sems((CHUNKS + 1,))]
    hbm = pl.BlockSpec(memory_space=pl.ANY)
    d_tokens, d_phi, d_first = pl.pallas_call(
        kernel,
        out_shape=[
            jax.ShapeDtypeStruct((m, wide), BF16),
            jax.ShapeDtypeStruct((fine, slots), F32),
            jax.ShapeDtypeStruct((wide, hid), BF16),
        ],
        in_specs=[hbm] * 7,
        out_specs=[hbm, pl.BlockSpec(memory_space=pltpu.VMEM), hbm],
        scratch_shapes=scratch,
        compiler_params=pltpu.CompilerParams(collective_id=0, has_side_effects=True, vmem_limit_bytes=VMEM_LIMIT),
    )(tokens[0], slot_params, slot_outputs[0], expert_inputs[0], w_in[0], w_out[0], cotangent[0])
    return (d_tokens[None], d_phi, d_first[None])


def solution(mesh):
    return jax.shard_map(
        per_device,
        mesh=mesh,
        in_specs=(
            P(("pair", "ep"), None, None),
            P(),
            P(("pair", "ep"), None, None),
            P("ep", None, None),
            P("ep", None, "pair"),
            P("ep", "pair", None),
            P(("pair", "ep"), None, None),
        ),
        out_specs=(P(("pair", "ep"), None, None), P(("pair", "ep"), None), P("ep", None, "pair")),
        check_vma=False,
    )
```

```python
import functools

import jax
import jax.numpy as jnp
from jax import lax
from jax.experimental import pallas as pl
from jax.experimental.pallas import tpu as pltpu
from jax.sharding import PartitionSpec as P

F32 = jnp.float32
BF16 = jnp.bfloat16
MESH = pl.DeviceIdType.MESH

NX, NY, NZ, NC = 2, 4, 8, 2
SPOTS = NX * NY * NC
PLANE = NY * NZ * NC
SLOTS = NX * PLANE
CHUNKS = 5
VMEM_LIMIT = 44 * 2**20

Z1, W1, W2, Z2, SW, SZ = range(6)


def dot_nn(a, b):
    return lax.dot_general(a, b, (((1,), (0,)), ((), ())), preferred_element_type=F32)


def dot_nt(a, b):
    return lax.dot_general(a, b, (((1,), (1,)), ((), ())), preferred_element_type=F32)


def dot_tn(a, b):
    return lax.dot_general(a, b, (((0,), (0,)), ((), ())), preferred_element_type=F32)


def log2(n):
    return n.bit_length() - 1


def digits(value, sizes):
    out = []
    for size in reversed(sizes[1:]):
        out.append(value & (size - 1))
        value = value >> log2(size)
    out.append(value)
    return out[::-1]


def number(values, sizes):
    total = None
    for value, size in zip(values, sizes):
        total = value if total is None else (total << log2(size)) + value
    return total


def one_hot(source, along, n):
    r = lax.broadcasted_iota(jnp.int32, (n, n), along)
    other = lax.broadcasted_iota(jnp.int32, (n, n), 1 - along)
    return jnp.where(source(r) == other, 1.0, 0.0).astype(BF16)


def slot_of_place(r):
    z, h, y, c = digits(r, (NZ, NX, NY, NC))
    return number((h, y, z, c), (NX, NY, NZ, NC))


def turn_source(r):
    spot, z = digits(r, (SPOTS, NZ))
    return number((z, spot), (NZ, SPOTS))


def image_source(r):
    xy, c, z = digits(r, (2 * NX * NY, NC, NZ))
    return number((xy, z, c), (2 * NX * NY, NZ, NC))


def column_source(fine, r):
    g = (r * (-(-(2**18) // fine))) >> 18
    xy, c, z = digits(g, (2 * NX * NY, NC, NZ))
    return number((xy, z, c), (2 * NX * NY, NZ, NC)) * fine + (r - g * fine)


def kernel(
    tok_h, phi_h, so_h, ei_h, win_h, wout_h, cot_h,
    dtok_o, dphi_o, dwin_o,
    tok, phi, so, ei, win, wout, cot,
    phip, sop, eiq, tokq, gate, act, dpre, disp, comb, dcomb,
    place, turn, sort,
    sendz, recvz, sendw, rows, sendw2, recvw2, sendz2, back,
    ddisp, dlog, senda, recva, sendb, recvb,
    send_sem, recv_sem, load_sem,
):
    wide = tok.shape[1]
    cols = wide // CHUNKS
    hid = win.shape[1]
    hcols = hid // CHUNKS
    fine = wide // (2 * SLOTS)
    half = wide // 2

    p = lax.axis_index("pair")
    e = lax.axis_index("ep")
    c = lax.rem(e, NC)
    z = lax.rem(lax.div(e, NC), NZ)
    y = lax.rem(lax.div(e, NC * NZ), NY)
    h = lax.div(e, PLANE)
    spot = (h * NY + y) * NC + c
    me = p * SPOTS + spot

    z_peers = []
    for k in (NZ // 2, *(j for i in range(NZ // 2 - 1, 0, -1) for j in (i, NZ - i))):
        other = lax.rem(z + k, NZ)
        z_peers.append((other, (p, h * PLANE + y * (NZ * NC) + other * NC + c)))
    w_peers = []
    for dy in (NY // 2, *(j for i in range(NY // 2 - 1, 0, -1) for j in (i, NY - i)), 0):
        for dh, dp in ((1, 0), (1, 1), (0, 1), (0, 0)):
            for dc in range(NC - 1, -1, -1):
                if (dy, dh, dp, dc) == (0, 0, 0, 0):
                    continue
                h2, y2, c2, p2 = lax.rem(h + dh, NX), lax.rem(y + dy, NY), lax.rem(c + dc, NC), lax.rem(p + dp, 2)
                spot2 = (h2 * NY + y2) * NC + c2
                w_peers.append((spot2, p2 * SPOTS + spot2, (p2, h2 * PLANE + y2 * (NZ * NC) + z * NC + c2)))

    def send(src, dst, step, ch, device):
        pltpu.make_async_remote_copy(
            src_ref=src, dst_ref=dst, send_sem=send_sem.at[step, ch], recv_sem=recv_sem.at[step, ch],
            device_id=device, device_id_type=MESH,
        ).start()

    def arrived(dst, step, ch):
        pltpu.make_async_copy(dst, dst, recv_sem.at[step, ch]).wait()

    def left(src, step, ch):
        pltpu.make_async_copy(src, src, send_sem.at[step, ch]).wait()

    def aligned(start, size):
        return pl.ds(pl.multiple_of(start, size), size)

    loads = [
        pltpu.make_async_copy(src, dst, load_sem.at[k])
        for k, (src, dst) in enumerate(
            [(tok_h, tok), (phi_h, phi), (cot_h, cot), (ei_h, ei), (win_h, win), (wout_h, wout), (so_h, so)]
        )
    ]
    for load in loads:
        load.start()
    load_tok, load_phi, load_cot, load_ei, load_win, load_wout, load_so = loads

    barrier = pltpu.get_barrier_semaphore()
    for peer in z_peers + w_peers:
        pl.semaphore_signal(barrier, inc=1, device_id=peer[-1], device_id_type=MESH)

    place[...] = one_hot(slot_of_place, 1, SLOTS)
    turn[...] = one_hot(turn_source, 0, SLOTS)

    load_phi.wait()
    phip[...] = dot_nn(phi[...], place[...]).astype(BF16)
    load_tok.wait()
    logits = dot_nn(tok[...], phip[...])
    over_tokens = jnp.exp(logits - jnp.max(logits, axis=0, keepdims=True))
    disp[...] = over_tokens / jnp.sum(over_tokens, axis=0, keepdims=True)
    over_slots = jnp.exp(logits - jnp.max(logits, axis=1, keepdims=True))
    combine = over_slots / jnp.sum(over_slots, axis=1, keepdims=True)
    comb[...] = combine
    combine_t = jnp.transpose(combine).astype(BF16)
    load_cot.wait()

    pl.semaphore_wait(barrier, len(z_peers) + len(w_peers))

    for ch in range(CHUNKS):
        d_slot_out = dot_nn(combine_t, cot[:, ch * cols : (ch + 1) * cols])
        sendz[ch] = d_slot_out.reshape(NZ, SPOTS, cols).astype(BF16)
        for other, device in z_peers:
            send(sendz.at[ch, other], recvz.at[ch, z], Z1, ch, device)
        recvz[ch, z] = sendz[ch, z]

    sort[...] = one_hot(image_source, 0, 2 * SLOTS)
    load_ei.wait()
    eiq[...] = dot_nn(sort[...], ei[...]).astype(BF16)
    load_win.wait()

    def pre_part(ch, _):
        span = aligned(ch * hcols, hcols)
        pre = dot_nn(eiq[...], win[:, span])
        cdf = 0.5 * (1.0 + lax.erf(pre * (0.5**0.5)))
        pdf = jnp.exp(-0.5 * pre * pre) * 0.3989422804014327
        gate[:, span] = cdf + pre * pdf
        return 0

    lax.fori_loop(0, CHUNKS, pre_part, 0)

    def z_arrives(ch, _):
        arrived(recvz.at[ch, pl.ds(0, NZ - 1)], Z1, ch)
        turned = dot_nn(turn[...], recvz[ch].reshape(SLOTS, cols))
        sendw[ch] = turned.reshape(SPOTS, NZ, cols).astype(BF16)
        for other, _, device in w_peers:
            send(sendw.at[ch, other], rows.at[ch, me], W1, ch, device)
        rows[ch, me] = sendw[ch, spot]
        return 0

    lax.fori_loop(0, CHUNKS, z_arrives, 0)
    act[...] = jnp.zeros_like(act)
    load_wout.wait()

    def rows_arrive(ch, _):
        arrived(rows.at[ch, pl.ds(0, 2 * SPOTS - 1)], W1, ch)
        grads = rows[ch].reshape(2 * SLOTS, cols)
        for k in range(CHUNKS):
            span = slice(k * hcols, (k + 1) * hcols)
            act[:, span] += dot_nt(grads, wout[span, aligned(ch * cols, cols)])
        return 0

    lax.fori_loop(0, CHUNKS, rows_arrive, 0)
    dpre[...] = (act[...] * gate[...]).astype(BF16)

    def rows_back(ch, _):
        part = dot_nt(dpre[...], win[aligned(ch * cols, cols), :])
        sendw2[ch] = part.reshape(2 * SPOTS, NZ, cols).astype(BF16)
        for _, other, device in w_peers:
            send(sendw2.at[ch, other], recvw2.at[ch, me], W2, ch, device)
        recvw2[ch, me] = sendw2[ch, me]
        return 0

    lax.fori_loop(0, CHUNKS, rows_back, 0)

    def dwin_part(ch, _):
        span = aligned(ch * cols, cols)
        for k in range(CHUNKS):
            wide_span = slice(k * hcols, (k + 1) * hcols)
            dwin_o[span, wide_span] = dot_tn(eiq[:, span], dpre[:, wide_span]).astype(BF16)
        return 0

    lax.fori_loop(0, CHUNKS, dwin_part, 0)

    def pair_arrives(ch, _):
        arrived(recvw2.at[ch, pl.ds(0, 2 * SPOTS - 1)], W2, ch)
        summed = recvw2[ch, 0:SPOTS].astype(F32) + recvw2[ch, SPOTS : 2 * SPOTS].astype(F32)
        turned = dot_tn(turn[...], summed.reshape(SLOTS, cols).astype(BF16))
        sendz2[ch] = turned.reshape(NZ, SPOTS, cols).astype(BF16)
        for other, device in z_peers:
            send(sendz2.at[ch, other], back.at[ch, z], Z2, ch, device)
        back[ch, z] = sendz2[ch, z]
        return 0

    lax.fori_loop(0, CHUNKS, pair_arrives, 0)

    load_so.wait()
    sop[...] = dot_tn(place[...], so[...]).astype(BF16)
    dcomb[...] = dot_nt(cot[...], sop[...])
    order = one_hot(functools.partial(column_source, fine), 1, half)
    for k in range(2):
        tokq[:, k * half : (k + 1) * half] = dot_nn(tok[:, k * half : (k + 1) * half], order).astype(BF16)
    ddisp[...] = jnp.zeros_like(ddisp)

    def z_arrives_back(ch, _):
        arrived(back.at[ch, pl.ds(0, NZ - 1)], Z2, ch)
        ddisp[...] += dot_nt(tok[:, aligned(ch * cols, cols)], back[ch].reshape(SLOTS, cols))
        return 0

    lax.fori_loop(0, CHUNKS, z_arrives_back, 0)

    d_disp = ddisp[...]
    d_comb = dcomb[...]
    dispatch = disp[...]
    combine = comb[...]
    d_logits = dispatch * (d_disp - jnp.sum(dispatch * d_disp, axis=0, keepdims=True))
    d_logits = d_logits + combine * (d_comb - jnp.sum(combine * d_comb, axis=1, keepdims=True))
    d_logits = d_logits.astype(BF16)
    dlog[...] = d_logits

    in_order = dot_nt(d_logits, place[...]).astype(BF16)
    senda[...] = dot_tn(tokq[...], in_order).reshape(2 * SPOTS, NZ * fine, SLOTS).astype(BF16)
    for _, other, device in w_peers:
        send(senda.at[other], recva.at[me], SW, 0, device)
    recva[me] = senda[me]

    dispatch_b = disp[...].astype(BF16)

    def d_tokens(ch, _):
        span = aligned(ch * cols, cols)
        dtok_o[:, span] = (
            dot_nn(dispatch_b, back[ch].reshape(SLOTS, cols)) + dot_nt(dlog[...], phip[span, :])
        ).astype(BF16)
        return 0

    lax.fori_loop(0, CHUNKS, d_tokens, 0)

    arrived(recva.at[pl.ds(0, 2 * SPOTS - 1)], SW, 0)
    summed = recva[0].astype(F32)
    for k in range(1, 2 * SPOTS):
        summed = summed + recva[k].astype(F32)
    sendb[...] = jnp.zeros_like(sendb)
    for k in range(NZ):
        sendb[k, 0:fine, :] = summed[k * fine : (k + 1) * fine, :]
    for other, device in z_peers:
        send(sendb.at[other], recvb.at[z], SZ, 0, device)
    recvb[z] = sendb[z]
    arrived(recvb.at[pl.ds(0, NZ - 1)], SZ, 0)
    total = recvb[0]
    for k in range(1, NZ):
        total = total + recvb[k]
    dphi_o[...] = total[0:fine, :]

    def sent(ch, _):
        left(sendz.at[ch, pl.ds(0, NZ - 1)], Z1, ch)
        left(rows.at[ch, pl.ds(0, 2 * SPOTS - 1)], W1, ch)
        left(sendw2.at[ch, pl.ds(0, 2 * SPOTS - 1)], W2, ch)
        left(sendz2.at[ch, pl.ds(0, NZ - 1)], Z2, ch)
        return 0

    lax.fori_loop(0, CHUNKS, sent, 0)
    left(senda.at[pl.ds(0, 2 * SPOTS - 1)], SW, 0)
    left(sendb.at[pl.ds(0, NZ - 1)], SZ, 0)


def write_out(dtok_i, dphi_i, dwin_i, dtok_o, dphi_o, dwin_o, sem):
    copies = [
        pltpu.make_async_copy(src, dst, sem.at[k])
        for k, (src, dst) in enumerate([(dwin_i, dwin_o), (dtok_i, dtok_o), (dphi_i, dphi_o)])
    ]
    for copy in copies:
        copy.start()
    for copy in copies:
        copy.wait()


def per_device(tokens, slot_params, slot_outputs, expert_inputs, w_in, w_out, cotangent):
    images, (m, wide), slots, hid = 2 * SLOTS, tokens.shape[1:], SLOTS, w_in.shape[2]
    cols = wide // CHUNKS
    fine = wide // images
    vmem = pltpu.VMEM
    scratch = [
        vmem((m, wide), BF16), vmem((wide, slots), BF16), vmem((slots, wide), BF16), vmem((images, wide), BF16),
        vmem((wide, hid), BF16), vmem((hid, wide), BF16), vmem((m, wide), BF16),
        vmem((wide, slots), BF16), vmem((slots, wide), BF16), vmem((images, wide), BF16), vmem((m, wide), BF16),
        vmem((images, hid), F32), vmem((images, hid), F32),
        vmem((images, hid), BF16), vmem((m, slots), F32), vmem((m, slots), F32), vmem((m, slots), F32),
        vmem((slots, slots), BF16), vmem((slots, slots), BF16), vmem((images, images), BF16),
    ]
    by_z = vmem((CHUNKS, NZ, SPOTS, cols), BF16)
    by_spot = vmem((CHUNKS, SPOTS, NZ, cols), BF16)
    by_device = vmem((CHUNKS, 2 * SPOTS, NZ, cols), BF16)
    scratch += [by_z, by_z, by_spot, by_device, by_device, by_device, by_z, by_z]
    scratch += [
        vmem((m, slots), F32), vmem((m, slots), BF16),
        vmem((2 * SPOTS, NZ * fine, slots), BF16), vmem((2 * SPOTS, NZ * fine, slots), BF16),
        vmem((NZ, 8, slots), F32), vmem((NZ, 8, slots), F32),
    ]
    sems = pltpu.SemaphoreType.DMA
    scratch += [sems((6, CHUNKS)), sems((6, CHUNKS)), sems((7,))]
    hbm = pl.BlockSpec(memory_space=pl.ANY)
    held = pl.BlockSpec(memory_space=pltpu.VMEM)
    shapes = [
        jax.ShapeDtypeStruct((m, wide), BF16),
        jax.ShapeDtypeStruct((fine, slots), F32),
        jax.ShapeDtypeStruct((wide, hid), BF16),
    ]
    args = (tokens[0], slot_params, slot_outputs[0], expert_inputs[0], w_in[0], w_out[0], cotangent[0])
    results = pl.pallas_call(
        kernel,
        out_shape=[pltpu.VMEM(shape.shape, shape.dtype) for shape in shapes],
        in_specs=[hbm] * 7,
        out_specs=[held] * 3,
        scratch_shapes=scratch,
        compiler_params=pltpu.CompilerParams(collective_id=0, has_side_effects=True, vmem_limit_bytes=VMEM_LIMIT),
    )(*[pltpu.with_memory_space_constraint(arg, pltpu.HBM) for arg in args])
    d_tokens, d_phi, d_first = pl.pallas_call(
        write_out,
        out_shape=shapes,
        in_specs=[hbm] * 3,
        out_specs=[hbm] * 3,
        scratch_shapes=[sems((3,))],
    )(*results)
    return (d_tokens[None], d_phi, d_first[None])


def solution(mesh):
    return jax.shard_map(
        per_device,
        mesh=mesh,
        in_specs=(
            P(("pair", "ep"), None, None),
            P(),
            P(("pair", "ep"), None, None),
            P("ep", None, None),
            P("ep", None, "pair"),
            P("ep", "pair", None),
            P(("pair", "ep"), None, None),
        ),
        out_specs=(P(("pair", "ep"), None, None), P(("pair", "ep"), None), P("ep", None, "pair")),
        check_vma=False,
    )
```

```python
import functools

import jax
import jax.numpy as jnp
from jax import lax
from jax.experimental import pallas as pl
from jax.experimental.pallas import tpu as pltpu
from jax.sharding import PartitionSpec as P

F32 = jnp.float32
BF16 = jnp.bfloat16
MESH = pl.DeviceIdType.MESH

NX, NY, NZ, NC = 2, 4, 8, 2
SPOTS = NX * NY * NC
PLANE = NY * NZ * NC
SLOTS = NX * PLANE
CHUNKS = 5
VMEM_LIMIT = 44 * 2**20

Z1, W1, W2, Z2, SW, SZ = range(6)


def dot_nn(a, b):
    return lax.dot_general(a, b, (((1,), (0,)), ((), ())), preferred_element_type=F32)


def dot_nt(a, b):
    return lax.dot_general(a, b, (((1,), (1,)), ((), ())), preferred_element_type=F32)


def dot_tn(a, b):
    return lax.dot_general(a, b, (((0,), (0,)), ((), ())), preferred_element_type=F32)


def log2(n):
    return n.bit_length() - 1


def digits(value, sizes):
    out = []
    for size in reversed(sizes[1:]):
        out.append(value & (size - 1))
        value = value >> log2(size)
    out.append(value)
    return out[::-1]


def number(values, sizes):
    total = None
    for value, size in zip(values, sizes):
        total = value if total is None else (total << log2(size)) + value
    return total


def one_hot(source, along, n):
    r = lax.broadcasted_iota(jnp.int32, (n, n), along)
    other = lax.broadcasted_iota(jnp.int32, (n, n), 1 - along)
    return jnp.where(source(r) == other, 1.0, 0.0).astype(BF16)


def slot_of_place(r):
    z, h, y, c = digits(r, (NZ, NX, NY, NC))
    return number((h, y, z, c), (NX, NY, NZ, NC))


def turn_source(r):
    spot, z = digits(r, (SPOTS, NZ))
    return number((z, spot), (NZ, SPOTS))


def image_source(r):
    xy, c, z = digits(r, (2 * NX * NY, NC, NZ))
    return number((xy, z, c), (2 * NX * NY, NZ, NC))


def column_source(fine, r):
    g = (r * (-(-(2**18) // fine))) >> 18
    xy, c, z = digits(g, (2 * NX * NY, NC, NZ))
    return number((xy, z, c), (2 * NX * NY, NZ, NC)) * fine + (r - g * fine)


def kernel(
    tok_h, phi_h, so_h, ei_h, win_h, wout_h, cot_h,
    dtok_o, dphi_o, dwin_o,
    tok, phi, so, ei, win, wout, cot,
    phip, sop, eiq, tokq, gate, act, dpre, disp, comb, dcomb,
    place, turn, sort,
    sendz, recvz, sendw, rows, sendw2, recvw2, sendz2, back,
    ddisp, dlog, senda, recva, sendb, recvb,
    send_sem, recv_sem, load_sem,
):
    wide = tok.shape[1]
    cols = wide // CHUNKS
    hid = win.shape[1]
    hcols = hid // CHUNKS
    fine = wide // (2 * SLOTS)
    half = wide // 2

    p = lax.axis_index("pair")
    e = lax.axis_index("ep")
    c = lax.rem(e, NC)
    z = lax.rem(lax.div(e, NC), NZ)
    y = lax.rem(lax.div(e, NC * NZ), NY)
    h = lax.div(e, PLANE)
    spot = (h * NY + y) * NC + c
    me = p * SPOTS + spot

    z_peers = []
    for k in (NZ // 2, *(j for i in range(NZ // 2 - 1, 0, -1) for j in (i, NZ - i))):
        other = lax.rem(z + k, NZ)
        z_peers.append((other, (p, h * PLANE + y * (NZ * NC) + other * NC + c)))
    w_peers = []
    for dy in (NY // 2, *(j for i in range(NY // 2 - 1, 0, -1) for j in (i, NY - i)), 0):
        for dh, dp in ((1, 0), (1, 1), (0, 1), (0, 0)):
            for dc in range(NC - 1, -1, -1):
                if (dy, dh, dp, dc) == (0, 0, 0, 0):
                    continue
                h2, y2, c2, p2 = lax.rem(h + dh, NX), lax.rem(y + dy, NY), lax.rem(c + dc, NC), lax.rem(p + dp, 2)
                spot2 = (h2 * NY + y2) * NC + c2
                w_peers.append((spot2, p2 * SPOTS + spot2, (p2, h2 * PLANE + y2 * (NZ * NC) + z * NC + c2)))

    def send(src, dst, step, ch, device):
        pltpu.make_async_remote_copy(
            src_ref=src, dst_ref=dst, send_sem=send_sem.at[step, ch], recv_sem=recv_sem.at[step, ch],
            device_id=device, device_id_type=MESH,
        ).start()

    def arrived(dst, step, ch):
        pltpu.make_async_copy(dst, dst, recv_sem.at[step, ch]).wait()

    def left(src, step, ch):
        pltpu.make_async_copy(src, src, send_sem.at[step, ch]).wait()

    def aligned(start, size):
        return pl.ds(pl.multiple_of(start, size), size)

    loads = [
        pltpu.make_async_copy(src, dst, load_sem.at[k])
        for k, (src, dst) in enumerate(
            [(tok_h, tok), (phi_h, phi), (cot_h, cot), (ei_h, ei), (win_h, win), (wout_h, wout), (so_h, so)]
        )
    ]
    for load in loads:
        load.start()
    load_tok, load_phi, load_cot, load_ei, load_win, load_wout, load_so = loads

    barrier = pltpu.get_barrier_semaphore()
    for peer in z_peers + w_peers:
        pl.semaphore_signal(barrier, inc=1, device_id=peer[-1], device_id_type=MESH)

    place[...] = one_hot(slot_of_place, 1, SLOTS)
    turn[...] = one_hot(turn_source, 0, SLOTS)

    load_phi.wait()
    phip[...] = dot_nn(phi[...], place[...]).astype(BF16)
    load_tok.wait()
    logits = dot_nn(tok[...], phip[...])
    over_tokens = jnp.exp(logits - jnp.max(logits, axis=0, keepdims=True))
    disp[...] = over_tokens / jnp.sum(over_tokens, axis=0, keepdims=True)
    over_slots = jnp.exp(logits - jnp.max(logits, axis=1, keepdims=True))
    combine = over_slots / jnp.sum(over_slots, axis=1, keepdims=True)
    comb[...] = combine
    combine_t = jnp.transpose(combine).astype(BF16)
    load_cot.wait()

    pl.semaphore_wait(barrier, len(z_peers) + len(w_peers))

    for ch in range(CHUNKS):
        d_slot_out = dot_nn(combine_t, cot[:, ch * cols : (ch + 1) * cols])
        sendz[ch] = d_slot_out.reshape(NZ, SPOTS, cols).astype(BF16)
        for other, device in z_peers:
            send(sendz.at[ch, other], recvz.at[ch, z], Z1, ch, device)
        recvz[ch, z] = sendz[ch, z]

    sort[...] = one_hot(image_source, 0, 2 * SLOTS)
    load_ei.wait()
    eiq[...] = dot_nn(sort[...], ei[...]).astype(BF16)
    load_win.wait()

    def pre_part(ch, _):
        span = aligned(ch * hcols, hcols)
        pre = dot_nn(eiq[...], win[:, span])
        cdf = 0.5 * (1.0 + lax.erf(pre * (0.5**0.5)))
        pdf = jnp.exp(-0.5 * pre * pre) * 0.3989422804014327
        gate[:, span] = cdf + pre * pdf
        return 0

    lax.fori_loop(0, CHUNKS, pre_part, 0)

    def z_arrives(ch, _):
        arrived(recvz.at[ch, pl.ds(0, NZ - 1)], Z1, ch)
        turned = dot_nn(turn[...], recvz[ch].reshape(SLOTS, cols))
        sendw[ch] = turned.reshape(SPOTS, NZ, cols).astype(BF16)
        for other, _, device in w_peers:
            send(sendw.at[ch, other], rows.at[ch, me], W1, ch, device)
        rows[ch, me] = sendw[ch, spot]
        return 0

    lax.fori_loop(0, CHUNKS, z_arrives, 0)
    act[...] = jnp.zeros_like(act)
    load_wout.wait()

    def rows_arrive(ch, _):
        arrived(rows.at[ch, pl.ds(0, 2 * SPOTS - 1)], W1, ch)
        grads = rows[ch].reshape(2 * SLOTS, cols)
        for k in range(CHUNKS):
            span = slice(k * hcols, (k + 1) * hcols)
            act[:, span] += dot_nt(grads, wout[span, aligned(ch * cols, cols)])
        return 0

    lax.fori_loop(0, CHUNKS, rows_arrive, 0)
    dpre[...] = (act[...] * gate[...]).astype(BF16)

    def rows_back(ch, _):
        part = dot_nt(dpre[...], win[aligned(ch * cols, cols), :])
        sendw2[ch] = part.reshape(2 * SPOTS, NZ, cols).astype(BF16)
        for _, other, device in w_peers:
            send(sendw2.at[ch, other], recvw2.at[ch, me], W2, ch, device)
        recvw2[ch, me] = sendw2[ch, me]
        return 0

    lax.fori_loop(0, CHUNKS, rows_back, 0)

    def dwin_part(ch, _):
        span = aligned(ch * cols, cols)
        for k in range(CHUNKS):
            wide_span = slice(k * hcols, (k + 1) * hcols)
            dwin_o[span, wide_span] = dot_tn(eiq[:, span], dpre[:, wide_span]).astype(BF16)
        return 0

    lax.fori_loop(0, CHUNKS, dwin_part, 0)

    def pair_arrives(ch, _):
        arrived(recvw2.at[ch, pl.ds(0, 2 * SPOTS - 1)], W2, ch)
        summed = recvw2[ch, 0:SPOTS].astype(F32) + recvw2[ch, SPOTS : 2 * SPOTS].astype(F32)
        turned = dot_tn(turn[...], summed.reshape(SLOTS, cols).astype(BF16))
        sendz2[ch] = turned.reshape(NZ, SPOTS, cols).astype(BF16)
        for other, device in z_peers:
            send(sendz2.at[ch, other], back.at[ch, z], Z2, ch, device)
        back[ch, z] = sendz2[ch, z]
        return 0

    lax.fori_loop(0, CHUNKS, pair_arrives, 0)

    load_so.wait()
    sop[...] = dot_tn(place[...], so[...]).astype(BF16)
    dcomb[...] = dot_nt(cot[...], sop[...])
    order = one_hot(functools.partial(column_source, fine), 1, half)
    for k in range(2):
        tokq[:, k * half : (k + 1) * half] = dot_nn(tok[:, k * half : (k + 1) * half], order).astype(BF16)
    ddisp[...] = jnp.zeros_like(ddisp)

    def z_arrives_back(ch, _):
        arrived(back.at[ch, pl.ds(0, NZ - 1)], Z2, ch)
        ddisp[...] += dot_nt(tok[:, aligned(ch * cols, cols)], back[ch].reshape(SLOTS, cols))
        return 0

    lax.fori_loop(0, CHUNKS, z_arrives_back, 0)

    d_disp = ddisp[...]
    d_comb = dcomb[...]
    dispatch = disp[...]
    combine = comb[...]
    d_logits = dispatch * (d_disp - jnp.sum(dispatch * d_disp, axis=0, keepdims=True))
    d_logits = d_logits + combine * (d_comb - jnp.sum(combine * d_comb, axis=1, keepdims=True))
    d_logits = d_logits.astype(BF16)
    dlog[...] = d_logits

    in_order = dot_nt(d_logits, place[...]).astype(BF16)
    senda[...] = dot_tn(tokq[...], in_order).reshape(2 * SPOTS, NZ * fine, SLOTS).astype(BF16)
    for _, other, device in w_peers:
        send(senda.at[other], recva.at[me], SW, 0, device)
    recva[me] = senda[me]

    dispatch_b = disp[...].astype(BF16)

    def d_tokens(ch, _):
        span = aligned(ch * cols, cols)
        dtok_o[:, span] = (
            dot_nn(dispatch_b, back[ch].reshape(SLOTS, cols)) + dot_nt(dlog[...], phip[span, :])
        ).astype(BF16)
        return 0

    lax.fori_loop(0, CHUNKS, d_tokens, 0)

    arrived(recva.at[pl.ds(0, 2 * SPOTS - 1)], SW, 0)
    summed = recva[0].astype(F32)
    for k in range(1, 2 * SPOTS):
        summed = summed + recva[k].astype(F32)
    sendb[...] = jnp.zeros_like(sendb)
    for k in range(NZ):
        sendb[k, 0:fine, :] = summed[k * fine : (k + 1) * fine, :]
    for other, device in z_peers:
        send(sendb.at[other], recvb.at[z], SZ, 0, device)
    recvb[z] = sendb[z]
    arrived(recvb.at[pl.ds(0, NZ - 1)], SZ, 0)
    total = recvb[0]
    for k in range(1, NZ):
        total = total + recvb[k]
    dphi_o[...] = total[0:fine, :]

    def sent(ch, _):
        left(sendz.at[ch, pl.ds(0, NZ - 1)], Z1, ch)
        left(rows.at[ch, pl.ds(0, 2 * SPOTS - 1)], W1, ch)
        left(sendw2.at[ch, pl.ds(0, 2 * SPOTS - 1)], W2, ch)
        left(sendz2.at[ch, pl.ds(0, NZ - 1)], Z2, ch)
        return 0

    lax.fori_loop(0, CHUNKS, sent, 0)
    left(senda.at[pl.ds(0, 2 * SPOTS - 1)], SW, 0)
    left(sendb.at[pl.ds(0, NZ - 1)], SZ, 0)


def write_out(dtok_i, dphi_i, dwin_i, dtok_o, dphi_o, dwin_o, sem):
    copies = [
        pltpu.make_async_copy(src, dst, sem.at[k])
        for k, (src, dst) in enumerate([(dwin_i, dwin_o), (dtok_i, dtok_o), (dphi_i, dphi_o)])
    ]
    for copy in copies:
        copy.start()
    for copy in copies:
        copy.wait()


def per_device(tokens, slot_params, slot_outputs, expert_inputs, w_in, w_out, cotangent):
    images, (m, wide), slots, hid = 2 * SLOTS, tokens.shape[1:], SLOTS, w_in.shape[2]
    cols = wide // CHUNKS
    fine = wide // images
    vmem = pltpu.VMEM
    scratch = [
        vmem((m, wide), BF16), vmem((wide, slots), BF16), vmem((slots, wide), BF16), vmem((images, wide), BF16),
        vmem((wide, hid), BF16), vmem((hid, wide), BF16), vmem((m, wide), BF16),
        vmem((wide, slots), BF16), vmem((slots, wide), BF16), vmem((images, wide), BF16), vmem((m, wide), BF16),
        vmem((images, hid), F32), vmem((images, hid), F32),
        vmem((images, hid), BF16), vmem((m, slots), F32), vmem((m, slots), F32), vmem((m, slots), F32),
        vmem((slots, slots), BF16), vmem((slots, slots), BF16), vmem((images, images), BF16),
    ]
    by_z = vmem((CHUNKS, NZ, SPOTS, cols), BF16)
    by_spot = vmem((CHUNKS, SPOTS, NZ, cols), BF16)
    by_device = vmem((CHUNKS, 2 * SPOTS, NZ, cols), BF16)
    scratch += [by_z, by_z, by_spot, by_device, by_device, by_device, by_z, by_z]
    scratch += [
        vmem((m, slots), F32), vmem((m, slots), BF16),
        vmem((2 * SPOTS, NZ * fine, slots), BF16), vmem((2 * SPOTS, NZ * fine, slots), BF16),
        vmem((NZ, 8, slots), F32), vmem((NZ, 8, slots), F32),
    ]
    sems = pltpu.SemaphoreType.DMA
    scratch += [sems((6, CHUNKS)), sems((6, CHUNKS)), sems((7,))]
    hbm = pl.BlockSpec(memory_space=pl.ANY)
    held = pl.BlockSpec(memory_space=pltpu.VMEM)
    shapes = [
        jax.ShapeDtypeStruct((m, wide), BF16),
        jax.ShapeDtypeStruct((fine, slots), F32),
        jax.ShapeDtypeStruct((wide, hid), BF16),
    ]
    args = (tokens[0], slot_params, slot_outputs[0], expert_inputs[0], w_in[0], w_out[0], cotangent[0])
    results = pl.pallas_call(
        kernel,
        out_shape=[pltpu.VMEM(shape.shape, shape.dtype) for shape in shapes],
        in_specs=[hbm] * 7,
        out_specs=[held] * 3,
        scratch_shapes=scratch,
        compiler_params=pltpu.CompilerParams(collective_id=0, has_side_effects=True, vmem_limit_bytes=VMEM_LIMIT),
    )(*[pltpu.with_memory_space_constraint(arg, pltpu.HBM) for arg in args])
    d_tokens, d_phi, d_first = pl.pallas_call(
        write_out,
        out_shape=shapes,
        in_specs=[hbm] * 3,
        out_specs=[hbm] * 3,
        scratch_shapes=[sems((3,))],
        compiler_params=pltpu.CompilerParams(vmem_limit_bytes=2**20),
    )(*[pltpu.with_memory_space_constraint(result, pltpu.VMEM) for result in results])
    return (d_tokens[None], d_phi, d_first[None])


def solution(mesh):
    return jax.shard_map(
        per_device,
        mesh=mesh,
        in_specs=(
            P(("pair", "ep"), None, None),
            P(),
            P(("pair", "ep"), None, None),
            P("ep", None, None),
            P("ep", None, "pair"),
            P("ep", "pair", None),
            P(("pair", "ep"), None, None),
        ),
        out_specs=(P(("pair", "ep"), None, None), P(("pair", "ep"), None), P("ep", None, "pair")),
        check_vma=False,
    )
```

```python
import functools

import jax
import jax.numpy as jnp
from jax import lax
from jax.experimental import pallas as pl
from jax.experimental.pallas import tpu as pltpu
from jax.sharding import PartitionSpec as P

F32 = jnp.float32
BF16 = jnp.bfloat16
MESH = pl.DeviceIdType.MESH

NX, NY, NZ, NC = 2, 4, 8, 2
SPOTS = NX * NY * NC
PLANE = NY * NZ * NC
SLOTS = NX * PLANE
TILE = 256
VMEM_LIMIT = 44 * 2**20

Z1, W1, W2, Z2, V1, M1, M2, V2, SW, SZ = range(10)


def dot_nn(a, b):
    return lax.dot_general(a, b, (((1,), (0,)), ((), ())), preferred_element_type=F32)


def dot_nt(a, b):
    return lax.dot_general(a, b, (((1,), (1,)), ((), ())), preferred_element_type=F32)


def dot_tn(a, b):
    return lax.dot_general(a, b, (((0,), (0,)), ((), ())), preferred_element_type=F32)


def log2(n):
    return n.bit_length() - 1


def digits(value, sizes):
    out = []
    for size in reversed(sizes[1:]):
        out.append(value & (size - 1))
        value = value >> log2(size)
    out.append(value)
    return out[::-1]


def number(values, sizes):
    total = None
    for value, size in zip(values, sizes):
        total = value if total is None else (total << log2(size)) + value
    return total


def one_hot(source, along, n):
    r = lax.broadcasted_iota(jnp.int32, (n, n), along)
    other = lax.broadcasted_iota(jnp.int32, (n, n), 1 - along)
    return jnp.where(source(r) == other, 1.0, 0.0).astype(BF16)


def slot_of_place(r):
    z, h, y, c = digits(r, (NZ, NX, NY, NC))
    return number((h, y, z, c), (NX, NY, NZ, NC))


def turn_source(r):
    spot, z = digits(r, (SPOTS, NZ))
    return number((z, spot), (NZ, SPOTS))


def swap_source(r):
    z, device = digits(r, (NZ, 2 * SPOTS))
    return number((device, z), (2 * SPOTS, NZ))


def image_source(r):
    xy, c, z = digits(r, (2 * NX * NY, NC, NZ))
    return number((xy, z, c), (2 * NX * NY, NZ, NC))


def column_source(fine, r):
    g = (r * (-(-(2**18) // fine))) >> 18
    xy, c, z = digits(g, (2 * NX * NY, NC, NZ))
    return number((xy, z, c), (2 * NX * NY, NZ, NC)) * fine + (r - g * fine)


def kernel(
    tok_h, phi_h, so_h, ei_h, win_h, wout_h, cot_h,
    dtok_o, dphi_o, dwin_o,
    tok, phi, so, ei, win, wout, cot,
    phip, sop, eiq, tokq, gate, act, dpre, disp, comb, dcomb,
    place, turn, sort, swap, combine_s,
    sendz, recvz, sendw, rows, sendw2, recvw2, sendz2, back,
    sendm, recvm, sendm2, recvm2,
    combine_t, ddisp, dlog, senda, recva, sendb, recvb,
    send_sem, recv_sem, load_sem,
):
    wide = tok.shape[1]
    hid = win.shape[1]
    pieces = hid // TILE
    fine = wide // (2 * SLOTS)
    half = wide // 2

    p = lax.axis_index("pair")
    e = lax.axis_index("ep")
    c = lax.rem(e, NC)
    z = lax.rem(lax.div(e, NC), NZ)
    y = lax.rem(lax.div(e, NC * NZ), NY)
    h = lax.div(e, PLANE)
    spot = (h * NY + y) * NC + c
    me = p * SPOTS + spot

    z_peers = []
    for k in (NZ // 2, *(j for i in range(NZ // 2 - 1, 0, -1) for j in (i, NZ - i))):
        other = lax.rem(z + k, NZ)
        z_peers.append((other, (p, h * PLANE + y * (NZ * NC) + other * NC + c)))
    w_peers = []
    for dy in (NY // 2, *(j for i in range(NY // 2 - 1, 0, -1) for j in (i, NY - i)), 0):
        for dh, dp in ((1, 0), (1, 1), (0, 1), (0, 0)):
            for dc in range(NC - 1, -1, -1):
                if (dy, dh, dp, dc) == (0, 0, 0, 0):
                    continue
                h2, y2, c2, p2 = lax.rem(h + dh, NX), lax.rem(y + dy, NY), lax.rem(c + dc, NC), lax.rem(p + dp, 2)
                spot2 = (h2 * NY + y2) * NC + c2
                w_peers.append((spot2, p2 * SPOTS + spot2, (p2, h2 * PLANE + y2 * (NZ * NC) + z * NC + c2)))

    def send(src, dst, step, ch, device):
        pltpu.make_async_remote_copy(
            src_ref=src, dst_ref=dst, send_sem=send_sem.at[step, ch], recv_sem=recv_sem.at[step, ch],
            device_id=device, device_id_type=MESH,
        ).start()

    def arrived(dst, step, ch):
        pltpu.make_async_copy(dst, dst, recv_sem.at[step, ch]).wait()

    def left(src, step, ch):
        pltpu.make_async_copy(src, src, send_sem.at[step, ch]).wait()

    def aligned(start, size):
        if isinstance(start, int):
            return pl.ds(start, size)
        return pl.ds(pl.multiple_of(start, size), size)

    half_tile = TILE // 2
    tail = pl.ds(3 * TILE, half_tile)
    mixed = pl.ds(3 * TILE + half_tile, 3 * half_tile)

    def whole_span(k):
        return aligned(k * TILE, TILE)

    def mixed_span(k):
        return aligned((7 + k) * half_tile, half_tile)

    def thrice(*steps):
        def body(k, _):
            for step, span_of in steps:
                step(span_of(k), k)
            return 0

        lax.fori_loop(0, 3, body, 0)

    barrier = pltpu.get_barrier_semaphore()
    for peer in z_peers + w_peers:
        pl.semaphore_signal(barrier, inc=1, device_id=peer[-1], device_id_type=MESH)

    loads = [
        pltpu.make_async_copy(src, dst, load_sem.at[k])
        for k, (src, dst) in enumerate(
            [(tok_h, tok), (phi_h, phi), (cot_h, cot), (ei_h, ei), (win_h, win), (wout_h, wout), (so_h, so)]
        )
    ]
    for load in loads:
        load.start()
    load_tok, load_phi, load_cot, load_ei, load_win, load_wout, load_so = loads

    place[...] = one_hot(slot_of_place, 1, SLOTS)
    turn[...] = one_hot(turn_source, 0, SLOTS)
    swap[...] = one_hot(swap_source, 0, 2 * SLOTS)

    load_phi.wait()
    phip[...] = dot_nn(phi[...], place[...]).astype(BF16)
    load_tok.wait()
    logits = dot_nn(tok[...], phip[...])
    over_tokens = jnp.exp(logits - jnp.max(logits, axis=0, keepdims=True))
    disp[...] = over_tokens / jnp.sum(over_tokens, axis=0, keepdims=True)
    over_slots = jnp.exp(logits - jnp.max(logits, axis=1, keepdims=True))
    combine = over_slots / jnp.sum(over_slots, axis=1, keepdims=True)
    comb[...] = combine
    combine_t[...] = jnp.transpose(combine).astype(BF16)
    combine_s[...] = dot_nn(turn[...], combine_t[...]).astype(BF16)
    load_cot.wait()

    pl.semaphore_wait(barrier, len(z_peers) + len(w_peers))

    def slot_grads(span, k):
        d_slot_out = dot_nn(combine_t[...], cot[:, span])
        sendz[:, :, span] = d_slot_out.reshape(NZ, SPOTS, span.size).astype(BF16)
        for other, device in z_peers:
            send(sendz.at[other, :, span], recvz.at[z, :, span], Z1, k, device)
        recvz[z, :, span] = sendz[z, :, span]

    def slot_grads_mixed(span, k):
        d_slot_out = dot_nn(combine_s[...], cot[:, span])
        sendw[:, :, span] = d_slot_out.reshape(SPOTS, NZ, span.size).astype(BF16)
        for other, _, device in w_peers:
            send(sendw.at[other, :, span], rows.at[me, :, span], V1, k, device)
        rows[me, :, span] = sendw[spot, :, span]

    thrice((slot_grads, whole_span), (slot_grads_mixed, mixed_span))
    slot_grads(tail, 3)

    sort[...] = one_hot(image_source, 0, 2 * SLOTS)
    load_ei.wait()
    eiq[...] = dot_nn(sort[...], ei[...]).astype(BF16)
    load_win.wait()

    def pre_part(k, _):
        span = aligned(k * TILE, TILE)
        pre = dot_nn(eiq[...], win[:, span])
        cdf = 0.5 * (1.0 + lax.erf(pre * (0.5**0.5)))
        pdf = jnp.exp(-0.5 * pre * pre) * 0.3989422804014327
        gate[:, span] = cdf + pre * pdf
        return 0

    lax.fori_loop(0, pieces, pre_part, 0)

    def z_arrives(span, k):
        arrived(recvz.at[pl.ds(0, NZ - 1), :, span], Z1, k)
        turned = dot_nn(turn[...], recvz[:, :, span].reshape(SLOTS, span.size))
        sendw[:, :, span] = turned.reshape(SPOTS, NZ, span.size).astype(BF16)
        for other, _, device in w_peers:
            send(sendw.at[other, :, span], rows.at[me, :, span], W1, k, device)
        rows[me, :, span] = sendw[spot, :, span]

    def v_arrives(span, k):
        arrived(rows.at[pl.ds(0, 2 * SPOTS - 1), :, span], V1, k)
        swapped = dot_nn(swap[...], rows[:, :, span].reshape(2 * SLOTS, span.size))
        sendm[:, :, span] = swapped.reshape(NZ, 2 * SPOTS, span.size).astype(BF16)
        for other, device in z_peers:
            send(sendm.at[other, :, span], recvm.at[z, :, span], M1, k, device)
        recvm[z, :, span] = sendm[z, :, span]

    thrice((z_arrives, whole_span), (v_arrives, mixed_span))
    z_arrives(tail, 3)

    act[...] = jnp.zeros_like(act)
    load_wout.wait()
    load_so.wait()
    sop[...] = dot_tn(place[...], so[...]).astype(BF16)
    dcomb[...] = dot_nt(cot[...], sop[...])
    order = one_hot(functools.partial(column_source, fine), 1, half)
    for k in range(2):
        tokq[:, k * half : (k + 1) * half] = dot_nn(tok[:, k * half : (k + 1) * half], order).astype(BF16)

    def add_to_act(grads, span):
        for j in range(pieces):
            part = slice(j * TILE, (j + 1) * TILE)
            act[:, part] += dot_nt(grads, wout[part, span])

    def rows_arrive(span, k):
        arrived(rows.at[pl.ds(0, 2 * SPOTS - 1), :, span], W1, k)
        add_to_act(rows[:, :, span].reshape(2 * SLOTS, span.size), span)

    thrice((rows_arrive, whole_span))
    for k in range(3):
        span = mixed_span(k)
        arrived(recvm.at[pl.ds(0, NZ - 1), :, span], M1, k)
    add_to_act(dot_tn(swap[...], recvm[:, :, mixed].reshape(2 * SLOTS, mixed.size)).astype(BF16), mixed)
    rows_arrive(tail, 3)
    dpre[...] = (act[...] * gate[...]).astype(BF16)

    def rows_back(span, k):
        part = dot_nt(dpre[...], win[span, :])
        sendw2[:, :, span] = part.reshape(2 * SPOTS, NZ, span.size).astype(BF16)
        for _, other, device in w_peers:
            send(sendw2.at[other, :, span], recvw2.at[me, :, span], W2, k, device)
        recvw2[me, :, span] = sendw2[me, :, span]

    def rows_back_mixed(span, k):
        part = dot_nt(dpre[...], win[span, :]).astype(BF16)
        sendm2[:, :, span] = dot_nn(swap[...], part).reshape(NZ, 2 * SPOTS, span.size).astype(BF16)
        for other, device in z_peers:
            send(sendm2.at[other, :, span], recvm2.at[z, :, span], M2, k, device)
        recvm2[z, :, span] = sendm2[z, :, span]

    rows_back(whole_span(0), 0)
    thrice((rows_back_mixed, mixed_span))
    rows_back(whole_span(1), 1)
    rows_back(whole_span(2), 2)
    rows_back(tail, 3)

    def dwin_part(k, _):
        span = aligned(k * TILE, TILE)
        for j in range(pieces):
            part = slice(j * TILE, (j + 1) * TILE)
            dwin_o[span, part] = dot_tn(eiq[:, span], dpre[:, part]).astype(BF16)
        return 0

    lax.fori_loop(0, wide // TILE, dwin_part, 0)
    ddisp[...] = jnp.zeros_like(ddisp)

    def m_arrives_back(span, k):
        arrived(recvm2.at[pl.ds(0, NZ - 1), :, span], M2, k)
        swapped = dot_tn(swap[...], recvm2[:, :, span].reshape(2 * SLOTS, span.size))
        sendw2[:, :, span] = swapped.reshape(2 * SPOTS, NZ, span.size).astype(BF16)
        for _, other, device in w_peers:
            send(sendw2.at[other, :, span], recvw2.at[me, :, span], V2, k, device)
        recvw2[me, :, span] = sendw2[me, :, span]

    def pair_sum(span):
        summed = recvw2[0:SPOTS, :, span].astype(F32) + recvw2[SPOTS : 2 * SPOTS, :, span].astype(F32)
        turned = dot_tn(turn[...], summed.reshape(SLOTS, span.size).astype(BF16))
        return turned.reshape(NZ, SPOTS, span.size).astype(BF16)

    def pair_arrives(span, k):
        arrived(recvw2.at[pl.ds(0, 2 * SPOTS - 1), :, span], W2, k)
        sendz2[:, :, span] = pair_sum(span)
        for other, device in z_peers:
            send(sendz2.at[other, :, span], back.at[z, :, span], Z2, k, device)
        back[z, :, span] = sendz2[z, :, span]

    thrice((pair_arrives, whole_span), (m_arrives_back, mixed_span))
    pair_arrives(tail, 3)

    def z_arrives_back(span, k):
        arrived(back.at[pl.ds(0, NZ - 1), :, span], Z2, k)
        ddisp[...] += dot_nt(tok[:, span], back[:, :, span].reshape(SLOTS, span.size))

    def v_arrives_back(span, k):
        arrived(recvw2.at[pl.ds(0, 2 * SPOTS - 1), :, span], V2, k)
        back[:, :, span] = pair_sum(span)

    thrice((z_arrives_back, whole_span))
    thrice((v_arrives_back, mixed_span))
    ddisp[...] += dot_nt(tok[:, mixed], back[:, :, mixed].reshape(SLOTS, mixed.size))
    z_arrives_back(tail, 3)

    d_disp = ddisp[...]
    d_comb = dcomb[...]
    dispatch = disp[...]
    combine = comb[...]
    d_logits = dispatch * (d_disp - jnp.sum(dispatch * d_disp, axis=0, keepdims=True))
    d_logits = d_logits + combine * (d_comb - jnp.sum(combine * d_comb, axis=1, keepdims=True))
    d_logits = d_logits.astype(BF16)
    dlog[...] = d_logits

    in_order = dot_nt(d_logits, place[...]).astype(BF16)
    senda[...] = dot_tn(tokq[...], in_order).reshape(2 * SPOTS, NZ * fine, SLOTS).astype(BF16)
    for _, other, device in w_peers:
        send(senda.at[other], recva.at[me], SW, 0, device)
    recva[me] = senda[me]

    dispatch_b = disp[...].astype(BF16)

    def d_tokens(k, _):
        span = aligned(k * TILE, TILE)
        dtok_o[:, span] = (
            dot_nn(dispatch_b, back[:, :, span].reshape(SLOTS, TILE)) + dot_nt(dlog[...], phip[span, :])
        ).astype(BF16)
        return 0

    lax.fori_loop(0, wide // TILE, d_tokens, 0)

    arrived(recva.at[pl.ds(0, 2 * SPOTS - 1)], SW, 0)
    summed = recva[0].astype(F32)
    for k in range(1, 2 * SPOTS):
        summed = summed + recva[k].astype(F32)
    sendb[...] = jnp.zeros_like(sendb)
    for k in range(NZ):
        sendb[k, 0:fine, :] = summed[k * fine : (k + 1) * fine, :]
    for other, device in z_peers:
        send(sendb.at[other], recvb.at[z], SZ, 0, device)
    recvb[z] = sendb[z]
    arrived(recvb.at[pl.ds(0, NZ - 1)], SZ, 0)
    total = recvb[0]
    for k in range(1, NZ):
        total = total + recvb[k]
    dphi_o[...] = total[0:fine, :]

    def sent(span, k):
        left(sendz.at[pl.ds(0, NZ - 1), :, span], Z1, k)
        left(rows.at[pl.ds(0, 2 * SPOTS - 1), :, span], W1, k)
        left(sendw2.at[pl.ds(0, 2 * SPOTS - 1), :, span], W2, k)
        left(sendz2.at[pl.ds(0, NZ - 1), :, span], Z2, k)

    def sent_mixed(span, k):
        left(rows.at[pl.ds(0, 2 * SPOTS - 1), :, span], V1, k)
        left(sendm.at[pl.ds(0, NZ - 1), :, span], M1, k)
        left(sendm2.at[pl.ds(0, NZ - 1), :, span], M2, k)
        left(recvw2.at[pl.ds(0, 2 * SPOTS - 1), :, span], V2, k)

    thrice((sent, whole_span), (sent_mixed, mixed_span))
    sent(tail, 3)
    left(senda.at[pl.ds(0, 2 * SPOTS - 1)], SW, 0)
    left(sendb.at[pl.ds(0, NZ - 1)], SZ, 0)


def write_out(dtok_i, dphi_i, dwin_i, dtok_o, dphi_o, dwin_o, sem):
    copies = [(dtok_i, dtok_o), (dphi_i, dphi_o)]
    n = dwin_i.shape[0] // 4
    copies += [(dwin_i.at[pl.ds(k * n, n)], dwin_o.at[pl.ds(k * n, n)]) for k in range(4)]
    copies = [pltpu.make_async_copy(src, dst, sem.at[k]) for k, (src, dst) in enumerate(copies)]
    for copy in copies:
        copy.start()
    for copy in copies:
        copy.wait()


def per_device(tokens, slot_params, slot_outputs, expert_inputs, w_in, w_out, cotangent):
    images, (m, wide), slots, hid = 2 * SLOTS, tokens.shape[1:], SLOTS, w_in.shape[2]
    fine = wide // images
    vmem = pltpu.VMEM
    scratch = [
        vmem((m, wide), BF16), vmem((wide, slots), BF16), vmem((slots, wide), BF16), vmem((images, wide), BF16),
        vmem((wide, hid), BF16), vmem((hid, wide), BF16), vmem((m, wide), BF16),
        vmem((wide, slots), BF16), vmem((slots, wide), BF16), vmem((images, wide), BF16), vmem((m, wide), BF16),
        vmem((images, hid), F32), vmem((images, hid), F32),
        vmem((images, hid), BF16), vmem((m, slots), F32), vmem((m, slots), F32), vmem((m, slots), F32),
        vmem((slots, slots), BF16), vmem((slots, slots), BF16), vmem((images, images), BF16),
        vmem((images, images), BF16), vmem((slots, m), BF16),
    ]
    by_z = vmem((NZ, SPOTS, wide), BF16)
    by_spot = vmem((SPOTS, NZ, wide), BF16)
    by_device = vmem((2 * SPOTS, NZ, wide), BF16)
    scratch += [by_z, by_z, by_spot, by_device, by_device, by_device, by_z, by_z]
    scratch += [vmem((NZ, 2 * SPOTS, wide), BF16)] * 4
    scratch += [
        vmem((slots, m), BF16), vmem((m, slots), F32), vmem((m, slots), BF16),
        vmem((2 * SPOTS, NZ * fine, slots), BF16), vmem((2 * SPOTS, NZ * fine, slots), BF16),
        vmem((NZ, 8, slots), F32), vmem((NZ, 8, slots), F32),
    ]
    sems = pltpu.SemaphoreType.DMA
    scratch += [sems((10, 4)), sems((10, 4)), sems((7,))]
    hbm = pl.BlockSpec(memory_space=pl.ANY)
    held = pl.BlockSpec(memory_space=pltpu.VMEM)
    shapes = [
        jax.ShapeDtypeStruct((m, wide), BF16),
        jax.ShapeDtypeStruct((fine, slots), F32),
        jax.ShapeDtypeStruct((wide, hid), BF16),
    ]
    args = (tokens[0], slot_params, slot_outputs[0], expert_inputs[0], w_in[0], w_out[0], cotangent[0])
    results = pl.pallas_call(
        kernel,
        out_shape=[pltpu.VMEM(shape.shape, shape.dtype) for shape in shapes],
        in_specs=[hbm] * 7,
        out_specs=[held] * 3,
        scratch_shapes=scratch,
        compiler_params=pltpu.CompilerParams(collective_id=0, has_side_effects=True, vmem_limit_bytes=VMEM_LIMIT),
    )(*[pltpu.with_memory_space_constraint(arg, pltpu.HBM) for arg in args])
    d_tokens, d_phi, d_first = pl.pallas_call(
        write_out,
        out_shape=shapes,
        in_specs=[hbm] * 3,
        out_specs=[hbm] * 3,
        scratch_shapes=[sems((6,))],
        compiler_params=pltpu.CompilerParams(vmem_limit_bytes=2**20),
    )(*[pltpu.with_memory_space_constraint(result, pltpu.VMEM) for result in results])
    return (d_tokens[None], d_phi, d_first[None])


def solution(mesh):
    return jax.shard_map(
        per_device,
        mesh=mesh,
        in_specs=(
            P(("pair", "ep"), None, None),
            P(),
            P(("pair", "ep"), None, None),
            P("ep", None, None),
            P("ep", None, "pair"),
            P("ep", "pair", None),
            P(("pair", "ep"), None, None),
        ),
        out_specs=(P(("pair", "ep"), None, None), P(("pair", "ep"), None), P("ep", None, "pair")),
        check_vma=False,
    )
```

```python
import functools

import jax
import jax.numpy as jnp
from jax import lax
from jax.experimental import pallas as pl
from jax.experimental.pallas import tpu as pltpu
from jax.sharding import PartitionSpec as P

F32 = jnp.float32
BF16 = jnp.bfloat16
MESH = pl.DeviceIdType.MESH

NX, NY, NZ, NC = 2, 4, 8, 2
SPOTS = NX * NY * NC
PLANE = NY * NZ * NC
SLOTS = NX * PLANE
TILE = 256
VMEM_LIMIT = 44 * 2**20

Z1, W1, W2, Z2, V1, M1, M2, V2, SW, SZ = range(10)


def dot_nn(a, b):
    return lax.dot_general(a, b, (((1,), (0,)), ((), ())), preferred_element_type=F32)


def dot_nt(a, b):
    return lax.dot_general(a, b, (((1,), (1,)), ((), ())), preferred_element_type=F32)


def dot_tn(a, b):
    return lax.dot_general(a, b, (((0,), (0,)), ((), ())), preferred_element_type=F32)


def log2(n):
    return n.bit_length() - 1


def digits(value, sizes):
    out = []
    for size in reversed(sizes[1:]):
        out.append(value & (size - 1))
        value = value >> log2(size)
    out.append(value)
    return out[::-1]


def number(values, sizes):
    total = None
    for value, size in zip(values, sizes):
        total = value if total is None else (total << log2(size)) + value
    return total


def one_hot(source, along, n):
    r = lax.broadcasted_iota(jnp.int32, (n, n), along)
    other = lax.broadcasted_iota(jnp.int32, (n, n), 1 - along)
    return jnp.where(source(r) == other, 1.0, 0.0).astype(BF16)


def slot_of_place(r):
    z, h, y, c = digits(r, (NZ, NX, NY, NC))
    return number((h, y, z, c), (NX, NY, NZ, NC))


def turn_source(r):
    spot, z = digits(r, (SPOTS, NZ))
    return number((z, spot), (NZ, SPOTS))


def swap_source(r):
    z, device = digits(r, (NZ, 2 * SPOTS))
    return number((device, z), (2 * SPOTS, NZ))


def image_source(r):
    xy, c, z = digits(r, (2 * NX * NY, NC, NZ))
    return number((xy, z, c), (2 * NX * NY, NZ, NC))


def column_source(fine, r):
    g = (r * (-(-(2**18) // fine))) >> 18
    xy, c, z = digits(g, (2 * NX * NY, NC, NZ))
    return number((xy, z, c), (2 * NX * NY, NZ, NC)) * fine + (r - g * fine)


def kernel(
    tok_h, phi_h, so_h, ei_h, win_h, wout_h, cot_h,
    dtok_o, dphi_o, dwin_o,
    tok, phi, so, ei, win, wout, cot,
    phip, sop, eiq, tokq, gate, act, dpre, disp, comb, dcomb,
    place, turn, sort, swap, combine_s,
    sendz, recvz, sendw, rows, sendw2, recvw2, sendz2, back,
    sendm, recvm, sendm2, recvm2,
    combine_t, ddisp, dlog, senda, recva, sendb, recvb,
    send_sem, recv_sem, load_sem,
):
    wide = tok.shape[1]
    hid = win.shape[1]
    pieces = hid // TILE
    fine = wide // (2 * SLOTS)
    half = wide // 2

    p = lax.axis_index("pair")
    e = lax.axis_index("ep")
    c = lax.rem(e, NC)
    z = lax.rem(lax.div(e, NC), NZ)
    y = lax.rem(lax.div(e, NC * NZ), NY)
    h = lax.div(e, PLANE)
    spot = (h * NY + y) * NC + c
    me = p * SPOTS + spot

    z_peers = []
    for k in (NZ // 2, *(j for i in range(NZ // 2 - 1, 0, -1) for j in (i, NZ - i))):
        other = lax.rem(z + k, NZ)
        z_peers.append((other, (p, h * PLANE + y * (NZ * NC) + other * NC + c)))
    w_peers = []
    for dy in (NY // 2, *(j for i in range(NY // 2 - 1, 0, -1) for j in (i, NY - i)), 0):
        for dh, dp in ((1, 0), (1, 1), (0, 1), (0, 0)):
            for dc in range(NC - 1, -1, -1):
                if (dy, dh, dp, dc) == (0, 0, 0, 0):
                    continue
                h2, y2, c2, p2 = lax.rem(h + dh, NX), lax.rem(y + dy, NY), lax.rem(c + dc, NC), lax.rem(p + dp, 2)
                spot2 = (h2 * NY + y2) * NC + c2
                w_peers.append((spot2, p2 * SPOTS + spot2, (p2, h2 * PLANE + y2 * (NZ * NC) + z * NC + c2)))

    def send(src, dst, step, ch, device):
        pltpu.make_async_remote_copy(
            src_ref=src, dst_ref=dst, send_sem=send_sem.at[step, ch], recv_sem=recv_sem.at[step, ch],
            device_id=device, device_id_type=MESH,
        ).start()

    def arrived(dst, step, ch):
        pltpu.make_async_copy(dst, dst, recv_sem.at[step, ch]).wait()

    def left(src, step, ch):
        pltpu.make_async_copy(src, src, send_sem.at[step, ch]).wait()

    def aligned(start, size):
        if isinstance(start, int):
            return pl.ds(start, size)
        return pl.ds(pl.multiple_of(start, size), size)

    half_tile = TILE // 2
    tail = pl.ds(3 * TILE, half_tile)
    mixed = pl.ds(3 * TILE + half_tile, 3 * half_tile)

    def whole_span(k):
        return aligned(k * TILE, TILE)

    def mixed_span(k):
        return aligned((7 + k) * half_tile, half_tile)

    def thrice(*steps):
        def body(k, _):
            for step, span_of in steps:
                step(span_of(k), k)
            return 0

        lax.fori_loop(0, 3, body, 0)

    barrier = pltpu.get_barrier_semaphore()
    for peer in z_peers + w_peers:
        pl.semaphore_signal(barrier, inc=1, device_id=peer[-1], device_id_type=MESH)

    loads = [
        pltpu.make_async_copy(src, dst, load_sem.at[k])
        for k, (src, dst) in enumerate(
            [(tok_h, tok), (phi_h, phi), (cot_h, cot), (ei_h, ei), (win_h, win), (wout_h, wout), (so_h, so)]
        )
    ]
    for load in loads:
        load.start()
    load_tok, load_phi, load_cot, load_ei, load_win, load_wout, load_so = loads

    place[...] = one_hot(slot_of_place, 1, SLOTS)
    turn[...] = one_hot(turn_source, 0, SLOTS)
    swap[...] = one_hot(swap_source, 0, 2 * SLOTS)

    load_phi.wait()
    phip[...] = dot_nn(phi[...], place[...]).astype(BF16)
    load_tok.wait()
    logits = dot_nn(tok[...], phip[...])
    over_tokens = jnp.exp(logits - jnp.max(logits, axis=0, keepdims=True))
    disp[...] = over_tokens / jnp.sum(over_tokens, axis=0, keepdims=True)
    over_slots = jnp.exp(logits - jnp.max(logits, axis=1, keepdims=True))
    combine = over_slots / jnp.sum(over_slots, axis=1, keepdims=True)
    comb[...] = combine
    combine_t[...] = jnp.transpose(combine).astype(BF16)
    combine_s[...] = dot_nn(turn[...], combine_t[...]).astype(BF16)
    load_cot.wait()

    pl.semaphore_wait(barrier, len(z_peers) + len(w_peers))

    def slot_grads(span, k):
        d_slot_out = dot_nn(combine_t[...], cot[:, span])
        sendz[:, :, span] = d_slot_out.reshape(NZ, SPOTS, span.size).astype(BF16)
        for other, device in z_peers:
            send(sendz.at[other, :, span], recvz.at[z, :, span], Z1, k, device)
        recvz[z, :, span] = sendz[z, :, span]

    def slot_grads_mixed(span, k):
        d_slot_out = dot_nn(combine_s[...], cot[:, span])
        sendw[:, :, span] = d_slot_out.reshape(SPOTS, NZ, span.size).astype(BF16)
        for other, _, device in w_peers:
            send(sendw.at[other, :, span], rows.at[me, :, span], V1, k, device)
        rows[me, :, span] = sendw[spot, :, span]

    thrice((slot_grads, whole_span), (slot_grads_mixed, mixed_span))
    slot_grads(tail, 3)

    sort[...] = one_hot(image_source, 0, 2 * SLOTS)
    load_ei.wait()
    eiq[...] = dot_nn(sort[...], ei[...]).astype(BF16)
    load_win.wait()

    def pre_part(k, _):
        span = aligned(k * TILE, TILE)
        pre = dot_nn(eiq[...], win[:, span])
        cdf = 0.5 * (1.0 + lax.erf(pre * (0.5**0.5)))
        pdf = jnp.exp(-0.5 * pre * pre) * 0.3989422804014327
        gate[:, span] = cdf + pre * pdf
        return 0

    lax.fori_loop(0, pieces, pre_part, 0)

    def z_arrives(span, k):
        arrived(recvz.at[pl.ds(0, NZ - 1), :, span], Z1, k)
        turned = dot_nn(turn[...], recvz[:, :, span].reshape(SLOTS, span.size))
        sendw[:, :, span] = turned.reshape(SPOTS, NZ, span.size).astype(BF16)
        for other, _, device in w_peers:
            send(sendw.at[other, :, span], rows.at[me, :, span], W1, k, device)
        rows[me, :, span] = sendw[spot, :, span]

    def v_arrives(span, k):
        arrived(rows.at[pl.ds(0, 2 * SPOTS - 1), :, span], V1, k)
        swapped = dot_nn(swap[...], rows[:, :, span].reshape(2 * SLOTS, span.size))
        sendm[:, :, span] = swapped.reshape(NZ, 2 * SPOTS, span.size).astype(BF16)
        for other, device in z_peers:
            send(sendm.at[other, :, span], recvm.at[z, :, span], M1, k, device)
        recvm[z, :, span] = sendm[z, :, span]

    thrice((z_arrives, whole_span), (v_arrives, mixed_span))
    z_arrives(tail, 3)

    act[...] = jnp.zeros_like(act)
    load_wout.wait()
    load_so.wait()
    sop[...] = dot_tn(place[...], so[...]).astype(BF16)
    dcomb[...] = dot_nt(cot[...], sop[...])
    order = one_hot(functools.partial(column_source, fine), 1, half)
    for k in range(2):
        tokq[:, k * half : (k + 1) * half] = dot_nn(tok[:, k * half : (k + 1) * half], order).astype(BF16)

    def add_to_act(grads, span):
        for j in range(pieces):
            part = slice(j * TILE, (j + 1) * TILE)
            act[:, part] += dot_nt(grads, wout[part, span])

    def rows_arrive(span, k):
        arrived(rows.at[pl.ds(0, 2 * SPOTS - 1), :, span], W1, k)
        add_to_act(rows[:, :, span].reshape(2 * SLOTS, span.size), span)

    thrice((rows_arrive, whole_span))
    for k in range(3):
        span = mixed_span(k)
        arrived(recvm.at[pl.ds(0, NZ - 1), :, span], M1, k)
    add_to_act(dot_tn(swap[...], recvm[:, :, mixed].reshape(2 * SLOTS, mixed.size)).astype(BF16), mixed)
    rows_arrive(tail, 3)
    dpre[...] = (act[...] * gate[...]).astype(BF16)

    def rows_back(span, k):
        part = dot_nt(dpre[...], win[span, :])
        sendw2[:, :, span] = part.reshape(2 * SPOTS, NZ, span.size).astype(BF16)
        for _, other, device in w_peers:
            send(sendw2.at[other, :, span], recvw2.at[me, :, span], W2, k, device)
        recvw2[me, :, span] = sendw2[me, :, span]

    def rows_back_mixed(span, k):
        part = dot_nt(dpre[...], win[span, :]).astype(BF16)
        sendm2[:, :, span] = dot_nn(swap[...], part).reshape(NZ, 2 * SPOTS, span.size).astype(BF16)
        for other, device in z_peers:
            send(sendm2.at[other, :, span], recvm2.at[z, :, span], M2, k, device)
        recvm2[z, :, span] = sendm2[z, :, span]

    rows_back(whole_span(0), 0)
    rows_back(whole_span(1), 1)
    thrice((rows_back_mixed, mixed_span))
    rows_back(whole_span(2), 2)
    rows_back(tail, 3)

    def dwin_part(k, _):
        span = aligned(k * TILE, TILE)
        for j in range(pieces):
            part = slice(j * TILE, (j + 1) * TILE)
            dwin_o[span, part] = dot_tn(eiq[:, span], dpre[:, part]).astype(BF16)
        return 0

    lax.fori_loop(0, wide // TILE, dwin_part, 0)
    ddisp[...] = jnp.zeros_like(ddisp)

    def m_arrives_back(span, k):
        arrived(recvm2.at[pl.ds(0, NZ - 1), :, span], M2, k)
        swapped = dot_tn(swap[...], recvm2[:, :, span].reshape(2 * SLOTS, span.size))
        sendw2[:, :, span] = swapped.reshape(2 * SPOTS, NZ, span.size).astype(BF16)
        for _, other, device in w_peers:
            send(sendw2.at[other, :, span], recvw2.at[me, :, span], V2, k, device)
        recvw2[me, :, span] = sendw2[me, :, span]

    def pair_sum(span):
        summed = recvw2[0:SPOTS, :, span].astype(F32) + recvw2[SPOTS : 2 * SPOTS, :, span].astype(F32)
        turned = dot_tn(turn[...], summed.reshape(SLOTS, span.size).astype(BF16))
        return turned.reshape(NZ, SPOTS, span.size).astype(BF16)

    def pair_arrives(span, k):
        arrived(recvw2.at[pl.ds(0, 2 * SPOTS - 1), :, span], W2, k)
        sendz2[:, :, span] = pair_sum(span)
        for other, device in z_peers:
            send(sendz2.at[other, :, span], back.at[z, :, span], Z2, k, device)
        back[z, :, span] = sendz2[z, :, span]

    thrice((pair_arrives, whole_span), (m_arrives_back, mixed_span))
    pair_arrives(tail, 3)

    def z_arrives_back(span, k):
        arrived(back.at[pl.ds(0, NZ - 1), :, span], Z2, k)
        ddisp[...] += dot_nt(tok[:, span], back[:, :, span].reshape(SLOTS, span.size))

    def v_arrives_back(span, k):
        arrived(recvw2.at[pl.ds(0, 2 * SPOTS - 1), :, span], V2, k)
        back[:, :, span] = pair_sum(span)

    thrice((z_arrives_back, whole_span))
    thrice((v_arrives_back, mixed_span))
    ddisp[...] += dot_nt(tok[:, mixed], back[:, :, mixed].reshape(SLOTS, mixed.size))
    z_arrives_back(tail, 3)

    d_disp = ddisp[...]
    d_comb = dcomb[...]
    dispatch = disp[...]
    combine = comb[...]
    d_logits = dispatch * (d_disp - jnp.sum(dispatch * d_disp, axis=0, keepdims=True))
    d_logits = d_logits + combine * (d_comb - jnp.sum(combine * d_comb, axis=1, keepdims=True))
    d_logits = d_logits.astype(BF16)
    dlog[...] = d_logits

    in_order = dot_nt(d_logits, place[...]).astype(BF16)
    senda[...] = dot_tn(tokq[...], in_order).reshape(2 * SPOTS, NZ * fine, SLOTS).astype(BF16)
    for _, other, device in w_peers:
        send(senda.at[other], recva.at[me], SW, 0, device)
    recva[me] = senda[me]

    dispatch_b = disp[...].astype(BF16)

    def d_tokens(k, _):
        span = aligned(k * TILE, TILE)
        dtok_o[:, span] = (
            dot_nn(dispatch_b, back[:, :, span].reshape(SLOTS, TILE)) + dot_nt(dlog[...], phip[span, :])
        ).astype(BF16)
        return 0

    lax.fori_loop(0, wide // TILE, d_tokens, 0)

    def sent(span, k):
        left(sendz.at[pl.ds(0, NZ - 1), :, span], Z1, k)
        left(rows.at[pl.ds(0, 2 * SPOTS - 1), :, span], W1, k)
        left(sendw2.at[pl.ds(0, 2 * SPOTS - 1), :, span], W2, k)
        left(sendz2.at[pl.ds(0, NZ - 1), :, span], Z2, k)

    def sent_mixed(span, k):
        left(rows.at[pl.ds(0, 2 * SPOTS - 1), :, span], V1, k)
        left(sendm.at[pl.ds(0, NZ - 1), :, span], M1, k)
        left(sendm2.at[pl.ds(0, NZ - 1), :, span], M2, k)
        left(recvw2.at[pl.ds(0, 2 * SPOTS - 1), :, span], V2, k)

    thrice((sent, whole_span), (sent_mixed, mixed_span))
    sent(tail, 3)

    arrived(recva.at[pl.ds(0, 2 * SPOTS - 1)], SW, 0)
    summed = recva[0].astype(F32)
    for k in range(1, 2 * SPOTS):
        summed = summed + recva[k].astype(F32)
    sendb[...] = jnp.zeros_like(sendb)
    for k in range(NZ):
        sendb[k, 0:fine, :] = summed[k * fine : (k + 1) * fine, :]
    for other, device in z_peers:
        send(sendb.at[other], recvb.at[z], SZ, 0, device)
    recvb[z] = sendb[z]
    left(senda.at[pl.ds(0, 2 * SPOTS - 1)], SW, 0)
    arrived(recvb.at[pl.ds(0, NZ - 1)], SZ, 0)
    total = recvb[0]
    for k in range(1, NZ):
        total = total + recvb[k]
    dphi_o[...] = total[0:fine, :]

    left(sendb.at[pl.ds(0, NZ - 1)], SZ, 0)


def write_out(dtok_i, dphi_i, dwin_i, dtok_o, dphi_o, dwin_o, sem):
    copies = [(dtok_i, dtok_o), (dphi_i, dphi_o)]
    n = dwin_i.shape[0] // 4
    copies += [(dwin_i.at[pl.ds(k * n, n)], dwin_o.at[pl.ds(k * n, n)]) for k in range(4)]
    copies = [pltpu.make_async_copy(src, dst, sem.at[k]) for k, (src, dst) in enumerate(copies)]
    for copy in copies:
        copy.start()
    for copy in copies:
        copy.wait()


def per_device(tokens, slot_params, slot_outputs, expert_inputs, w_in, w_out, cotangent):
    images, (m, wide), slots, hid = 2 * SLOTS, tokens.shape[1:], SLOTS, w_in.shape[2]
    fine = wide // images
    vmem = pltpu.VMEM
    scratch = [
        vmem((m, wide), BF16), vmem((wide, slots), BF16), vmem((slots, wide), BF16), vmem((images, wide), BF16),
        vmem((wide, hid), BF16), vmem((hid, wide), BF16), vmem((m, wide), BF16),
        vmem((wide, slots), BF16), vmem((slots, wide), BF16), vmem((images, wide), BF16), vmem((m, wide), BF16),
        vmem((images, hid), F32), vmem((images, hid), F32),
        vmem((images, hid), BF16), vmem((m, slots), F32), vmem((m, slots), F32), vmem((m, slots), F32),
        vmem((slots, slots), BF16), vmem((slots, slots), BF16), vmem((images, images), BF16),
        vmem((images, images), BF16), vmem((slots, m), BF16),
    ]
    by_z = vmem((NZ, SPOTS, wide), BF16)
    by_spot = vmem((SPOTS, NZ, wide), BF16)
    by_device = vmem((2 * SPOTS, NZ, wide), BF16)
    scratch += [by_z, by_z, by_spot, by_device, by_device, by_device, by_z, by_z]
    scratch += [vmem((NZ, 2 * SPOTS, wide), BF16)] * 4
    scratch += [
        vmem((slots, m), BF16), vmem((m, slots), F32), vmem((m, slots), BF16),
        vmem((2 * SPOTS, NZ * fine, slots), BF16), vmem((2 * SPOTS, NZ * fine, slots), BF16),
        vmem((NZ, 8, slots), F32), vmem((NZ, 8, slots), F32),
    ]
    sems = pltpu.SemaphoreType.DMA
    scratch += [sems((10, 4)), sems((10, 4)), sems((7,))]
    hbm = pl.BlockSpec(memory_space=pl.ANY)
    held = pl.BlockSpec(memory_space=pltpu.VMEM)
    shapes = [
        jax.ShapeDtypeStruct((m, wide), BF16),
        jax.ShapeDtypeStruct((fine, slots), F32),
        jax.ShapeDtypeStruct((wide, hid), BF16),
    ]
    args = (tokens[0], slot_params, slot_outputs[0], expert_inputs[0], w_in[0], w_out[0], cotangent[0])
    results = pl.pallas_call(
        kernel,
        out_shape=[pltpu.VMEM(shape.shape, shape.dtype) for shape in shapes],
        in_specs=[hbm] * 7,
        out_specs=[held] * 3,
        scratch_shapes=scratch,
        compiler_params=pltpu.CompilerParams(collective_id=0, has_side_effects=True, vmem_limit_bytes=VMEM_LIMIT),
    )(*[pltpu.with_memory_space_constraint(arg, pltpu.HBM) for arg in args])
    d_tokens, d_phi, d_first = pl.pallas_call(
        write_out,
        out_shape=shapes,
        in_specs=[hbm] * 3,
        out_specs=[hbm] * 3,
        scratch_shapes=[sems((6,))],
        compiler_params=pltpu.CompilerParams(vmem_limit_bytes=2**20),
    )(*[pltpu.with_memory_space_constraint(result, pltpu.VMEM) for result in results])
    return (d_tokens[None], d_phi, d_first[None])


def solution(mesh):
    return jax.shard_map(
        per_device,
        mesh=mesh,
        in_specs=(
            P(("pair", "ep"), None, None),
            P(),
            P(("pair", "ep"), None, None),
            P("ep", None, None),
            P("ep", None, "pair"),
            P("ep", "pair", None),
            P(("pair", "ep"), None, None),
        ),
        out_specs=(P(("pair", "ep"), None, None), P(("pair", "ep"), None), P("ep", None, "pair")),
        check_vma=False,
    )
```
